32 devices in a mesh: rollout: 2 (over core), context: 4 (over z), head: 4 (over y, x).
Axes of the slice: x: 2, y: 2, z: 4, core: 2. Of those that a mesh axis runs over, the one named last changes fastest.
Arguments:
- inner_raw: bfloat16 [2048, 8192], P(('rollout', 'context', 'head')), parts along dimension 0, may hold values from -6 to 6
- pairs_raw: bfloat16 [2048, 8, 2, 128], P(('rollout', 'context', 'head')), parts along dimension 0, may hold values from -2.5 to 2.5
- gate_raw: bfloat16 [2048, 8192], P(('rollout', 'context'), 'head'), parts along dimension 0, may hold values from -6 to 6
- step_raw: bfloat16 [2048, 128], P(('rollout', 'context'), 'head'), parts along dimension 0, may hold values from -3 to 3
- step_bias: float32 [128], P('head'), may hold values from -0.5 to 0.5
- rate_log: float32 [128], P('head'), may hold values from -13.5 to -2.8, as said below
- skip_gain: float32 [128], P('head'), may hold values from 0.5 to 2
- conv_inner: float32 [5, 8192], replicated, may hold values from -2.5 to 2.5
- conv_pairs: float32 [5, 8, 2, 128], replicated, may hold values from -2.5 to 2.5
- norm_gain: float32 [8192], P('head'), may hold values from 0.5 to 1.5
Outputs:
- mixer_out: bfloat16 [2048, 8192], P(('rollout', 'context', 'head')), parts along dimension 0
The draws below stay inside these ranges and needn't reach their ends.
There are 2 independent parts, one for each index of `rollout`. The reference program is written for one: setup_inputs(seed, part) draws one part's arguments, and reference() takes and returns one part's arrays. A program takes and returns all parts, laid end to end along the dimension named above; an argument that names none is the same for every part. Nothing has to cross between parts.
Inputs may be any that keep to these rules, and one draw needn't show every extreme that they name: `rate_log`: one value a head.
All inputs are finite; a program needn't handle non-finite values.
Results may differ from the reference program's by a relative error of at most 0.012.
The reference program's roundings to bfloat16 on the way (of `inner_conv`) count: a program that leaves them out, or rounds other values in their place, can miss the bound.
Values may be sent and summed in bfloat16 or wider, within the bound.
A program may use at most 128 MiB of HBM per device.

```python
import jax
import jax.numpy as jnp
from jax import lax

D_INNER = 8192
HEADS = 128
HEAD_DIM = 64
STATE = 128
GROUPS = 8
CONV = 4
BLOCK = 256
SEQ = 1024


def draw_rate_log(key, part):
    pick_key = jax.random.fold_in(key, 11)
    level_key = jax.random.fold_in(key, 12)
    slow_share = 0.5
    slow_heads = jax.random.uniform(pick_key, (HEADS,), jnp.float32) < slow_share
    level = jax.random.uniform(level_key, (HEADS,), jnp.float32)
    slow_rate = jnp.log(0.2 / SEQ) + level * jnp.log(5.0)
    fast_rate = jnp.log(0.02) + level * jnp.log(3.0)
    return jnp.where(slow_heads, slow_rate, fast_rate).astype(jnp.float32)


def levels(key, shape, pieces, smallest, largest):
    def one(position, shards_of):
        steps = jax.random.uniform(jax.random.fold_in(jax.random.fold_in(key, 6), position), (shards_of,), jnp.float32, smallest / len(pieces), largest / len(pieces))
        return jnp.repeat(jnp.exp(steps), shape[position] // shards_of).reshape((-1,) + (1,) * (len(shape) - position - 1))

    gain = one(*pieces[0])
    for cut in pieces[1:]:
        gain = gain * one(*cut)
    return gain


def noise(rng, shape, width, reach, shards=(), dtype=jnp.bfloat16):
    array = jax.random.normal(rng, shape, jnp.float32) * width
    if len(shards) > 0:
        array = levels(rng, shape, shards, -0.22, 0.18) * array
    return jnp.clip(array, min=-reach, max=reach).astype(dtype)


def setup_inputs(seed: int = 0, part: int = 0) -> dict:
    streams_of = jax.random.split(jax.random.key(seed), 11)
    part_keys = jax.random.split(jax.random.fold_in(streams_of[10], part), 11)
    inner_raw = noise(part_keys[0], (SEQ, D_INNER), 1.0, 6.0, ((0, 16),))
    pairs_raw = noise(part_keys[1], (SEQ, GROUPS, 2, STATE), 0.35, 2.5, ((0, 16),))
    gate_raw = noise(part_keys[2], (SEQ, D_INNER), 1.0, 6.0, ((0, 4), (1, 4)))
    step_raw = noise(part_keys[3], (SEQ, HEADS), 0.5, 3.0, ((0, 4), (1, 4)))
    step_bias = jnp.clip(jax.random.uniform(streams_of[4], (HEADS,), jnp.float32, -0.5, 0.5) * levels(streams_of[4], (HEADS,), ((0, 4),), -0.4, 0.0), -0.5, 0.5)
    rate_log = draw_rate_log(jax.random.fold_in(streams_of[10], 71), part)
    skip_gain = jnp.clip(0.5 + 1.5 * jax.random.uniform(streams_of[6], (HEADS,), jnp.float32) ** levels(streams_of[6], (HEADS,), ((0, 4),), -0.2, 0.2), 0.5, 2.0)
    conv_inner = noise(streams_of[7], (CONV + 1, D_INNER), 0.5, 2.5, (), jnp.float32)
    conv_pairs = noise(streams_of[8], (CONV + 1, GROUPS, 2, STATE), 0.5, 2.5, (), jnp.float32)
    norm_gain = jnp.clip(1.0 + 0.1 * jax.random.normal(streams_of[9], (D_INNER,), jnp.float32), 0.5, 1.5)
    return dict(inner_raw=inner_raw, pairs_raw=pairs_raw, gate_raw=gate_raw, step_raw=step_raw, step_bias=step_bias, rate_log=rate_log, skip_gain=skip_gain, conv_inner=conv_inner, conv_pairs=conv_pairs, norm_gain=norm_gain)


def convolve(raw_rows, before, weight):
    tap_count = weight.shape[0] - 1
    row_count = raw_rows.shape[0]
    extended = jnp.concatenate([before, raw_rows], axis=0).astype(jnp.float32)
    summed = weight[tap_count][None, :] + weight[0][None, :] * extended[0:row_count]
    for offset in range(1, tap_count):
        summed = summed + weight[offset][None, :] * extended[offset:offset + row_count]
    return jax.nn.silu(summed).astype(jnp.bfloat16)

def block_intra(inner_conv, pairs_conv, step_size, log_cum, groups):
    block_len, head_count = step_size.shape
    per_group = head_count // groups
    head_width = inner_conv.shape[1] // head_count
    pair_view = pairs_conv.reshape(block_len, groups, 2, -1).astype(jnp.float32)
    scores = jnp.einsum('ign,jgn->gij', pair_view[:, :, 1], pair_view[:, :, 0])
    lower_tri = lax.broadcasted_iota(jnp.int32, (block_len, block_len), 0) >= lax.broadcasted_iota(jnp.int32, (block_len, block_len), 1)
    cum_t = log_cum.T
    log_gap = jnp.minimum(cum_t[:, :, None] - cum_t[:, None, :], 0.0)
    decay_mat = jnp.where(lower_tri[None], jnp.exp(log_gap), 0.0) * step_size.T[:, None, :]
    weights = (scores[:, None] * decay_mat.reshape(groups, per_group, block_len, block_len)).astype(jnp.bfloat16)
    inner_view = inner_conv.reshape(block_len, groups, per_group, head_width).astype(jnp.float32)
    intra_out = jnp.einsum('gkij,jgkp->igkp', weights.astype(jnp.float32), inner_view)
    return intra_out.reshape(block_len, head_count * head_width)

def block_state(inner_conv, pairs_conv, step_size, log_cum, groups):
    block_len, head_count = step_size.shape
    per_group = head_count // groups
    head_width = inner_conv.shape[1] // head_count
    tail_w = jnp.exp(log_cum[-1][None, :] - log_cum) * step_size
    weighted = (inner_conv.reshape(block_len, head_count, head_width).astype(jnp.float32) * tail_w[:, :, None]).astype(jnp.bfloat16)
    weighted = weighted.reshape(block_len, groups, per_group, head_width)
    bmat = pairs_conv.reshape(block_len, groups, 2, -1)[:, :, 0]
    local_state = jnp.einsum('jgn,jgkp->gknp', bmat.astype(jnp.float32), weighted.astype(jnp.float32))
    return (local_state.reshape(head_count, -1, head_width), jnp.exp(log_cum[-1]))

def finish(inner_conv, pairs_conv, gate_rows, intra_out, carry_state, log_cum, skip_gain, norm_gain, groups):
    block_len, head_count = log_cum.shape
    per_group = head_count // groups
    head_width = inner_conv.shape[1] // head_count
    cmat = pairs_conv.reshape(block_len, groups, 2, -1)[:, :, 1]
    held = carry_state.astype(jnp.bfloat16).reshape(groups, per_group, -1, head_width)
    carried = jnp.einsum('ign,gknp->igkp', cmat.astype(jnp.float32), held.astype(jnp.float32))
    carried = carried.reshape(block_len, head_count, head_width) * jnp.exp(log_cum)[:, :, None]
    mixed = intra_out + carried.reshape(block_len, -1) + jnp.repeat(skip_gain, head_width)[None, :] * inner_conv.astype(jnp.float32)
    gated_out = mixed * jax.nn.silu(gate_rows.astype(jnp.float32))
    grouped = gated_out.reshape(block_len, groups, -1)
    inv_rms = lax.rsqrt(lax.optimization_barrier(jnp.mean(grouped * grouped, axis=2, keepdims=True)) + 1e-05)
    return ((grouped * inv_rms).reshape(block_len, -1) * norm_gain[None, :]).astype(jnp.bfloat16)

def reference(inner_raw, pairs_raw, gate_raw, step_raw, step_bias, rate_log, skip_gain, conv_inner, conv_pairs, norm_gain):
    tap_count = conv_inner.shape[0] - 1
    block_count = SEQ // BLOCK
    pairs_flat = pairs_raw.reshape(SEQ, -1)
    conv_flat = conv_pairs.reshape(tap_count + 1, -1)
    blocks = (inner_raw.reshape(block_count, BLOCK, D_INNER), pairs_flat.reshape(block_count, BLOCK, -1), gate_raw.reshape(block_count, BLOCK, D_INNER), step_raw.reshape(block_count, BLOCK, HEADS))

    def advance(running, element):
        carry_state, tail_inner, tail_pairs = running
        inner_rows, pair_rows, gate_rows, step_rows = element
        inner_conv = convolve(inner_rows, tail_inner, conv_inner)
        pairs_conv = convolve(pair_rows, tail_pairs, conv_flat)
        step_size = jax.nn.softplus(step_rows.astype(jnp.float32) + step_bias[None, :])
        log_cum = jnp.cumsum(-jnp.exp(rate_log)[None, :] * step_size, axis=0)
        intra_out = block_intra(inner_conv, pairs_conv, step_size, log_cum, GROUPS)
        local_state, block_decay = block_state(inner_conv, pairs_conv, step_size, log_cum, GROUPS)
        result = finish(inner_conv, pairs_conv, gate_rows, intra_out, carry_state, log_cum, skip_gain, norm_gain, GROUPS)
        carry_state = block_decay[:, None, None] * carry_state + local_state
        return ((carry_state, inner_rows[BLOCK - tap_count:], pair_rows[BLOCK - tap_count:]), result)
    start = (jnp.zeros((HEADS, STATE, HEAD_DIM), jnp.float32), jnp.zeros((tap_count, D_INNER), jnp.bfloat16), jnp.zeros((tap_count, pairs_flat.shape[1]), jnp.bfloat16))
    _, results = lax.scan(advance, start, blocks)
    return results.reshape(SEQ, D_INNER)
```

```python
import functools

import jax
import jax.numpy as jnp
from jax import lax
from jax.experimental import pallas as pl
from jax.experimental.pallas import tpu as pltpu
from jax.sharding import PartitionSpec as P

BLOCK = 256
PAD = 16
CHUNK = 32
WIDE = 256
BF = jnp.bfloat16
F32 = jnp.float32


def silu(v):
    return v / (1.0 + jnp.exp(-v))


def conv_rows(src, dst, weight, first_col, cols, dst_of):
    rows = src.shape[0] - PAD
    taps = weight.shape[0] - 1

    def step(i, carry):
        r0 = pl.multiple_of(i * CHUNK, CHUNK)
        for c0 in range(0, cols, WIDE):
            raw = src[pl.ds(r0, CHUNK + PAD), c0 : c0 + WIDE].astype(F32)
            w = weight[:, pl.ds(pl.multiple_of(first_col + c0, WIDE), WIDE)]
            total = w[taps : taps + 1]
            for k in range(taps):
                o = PAD - taps + k
                total = total + w[k : k + 1] * raw[o : o + CHUNK]
            dst_of(dst, r0, c0, silu(total).astype(BF))
        return carry

    lax.fori_loop(0, rows // CHUNK, step, 0)


def store_plain(dst, r0, c0, value):
    dst[pl.ds(r0, CHUNK), c0 : c0 + WIDE] = value


def kernel(
    n, nctx, groups, heads_local,
    inner, pairs, gate, step_raw, step_bias, rate_log, skip_gain, w_inner, w_pairs, norm_gain,
    out,
    xraw, praw, xc, pc, mixed, ex, local, scores, cin, cout, outbuf,
    xs, xr, ps, pr, lsem, hs, hr, cs, cr, os, orr, olsem,
):
    me = lax.axis_index("head")
    ctx = lax.axis_index("context")
    rows = inner.shape[0]
    width = gate.shape[1]
    gw = width // groups
    per = heads_local // groups
    hd = width // heads_local
    pw = praw.shape[1]
    st = pw // (2 * groups)
    pieces = gw // WIDE

    barrier = pltpu.get_barrier_semaphore()
    for k in range(1, n):
        pl.semaphore_signal(barrier, inc=1, device_id={"head": lax.rem(me + k, n)})

    @pl.when(ctx > 0)
    def _():
        pl.semaphore_signal(barrier, inc=1, device_id={"context": ctx - 1})

    @pl.when(ctx < nctx - 1)
    def _():
        pl.semaphore_signal(barrier, inc=1, device_id={"context": ctx + 1})

    links = jnp.where(ctx > 0, 1, 0) + jnp.where(ctx < nctx - 1, 1, 0)
    pl.semaphore_wait(barrier, n - 1 + links)

    def p_copy(k, who, at):
        return pltpu.make_async_remote_copy(
            src_ref=pairs.at[:, pl.ds(pl.multiple_of(who * pw, 128), pw)],
            dst_ref=praw.at[pl.ds(pl.multiple_of(PAD + at * rows, 16), rows), :],
            send_sem=ps.at[k - 1], recv_sem=pr.at[k - 1], device_id={"head": who})

    def x_copy(g, k, who, at):
        return pltpu.make_async_remote_copy(
            src_ref=inner.at[:, pl.ds(pl.multiple_of(who * width + g * gw, 128), gw)],
            dst_ref=xraw.at[g, pl.ds(pl.multiple_of(PAD + at * rows, 16), rows), :],
            send_sem=xs.at[g, k - 1], recv_sem=xr.at[g, k - 1], device_id={"head": who})

    def o_copy(g, k, who, at):
        return pltpu.make_async_remote_copy(
            src_ref=outbuf.at[g, pl.ds(pl.multiple_of(who * rows, 16), rows), :],
            dst_ref=out.at[:, pl.ds(pl.multiple_of(at * width + g * gw, 128), gw)],
            send_sem=os.at[g, k - 1], recv_sem=orr.at[g, k - 1], device_id={"head": who})

    def halo(i, ref):
        last = ref.shape[0] - PAD
        return pltpu.make_async_remote_copy(
            src_ref=ref.at[last:, :], dst_ref=ref.at[0:PAD, :],
            send_sem=hs.at[i], recv_sem=hr.at[i],
            device_id={"context": lax.rem(ctx + 1, nctx)})

    def chain(g, p):
        return pltpu.make_async_remote_copy(
            src_ref=cout.at[g, p], dst_ref=cin.at[g, p],
            send_sem=cs.at[g, p], recv_sem=cr.at[g, p],
            device_id={"context": lax.rem(ctx + 1, nctx)})

    def to(k):
        return lax.rem(me + k, n)

    def source(k):
        return lax.rem(me + n - k, n)

    for k in range(1, n):
        p_copy(k, to(k), me).start()
    for g in range(groups):
        for k in range(1, n):
            x_copy(g, k, to(k), me).start()
    own_rows = pl.ds(pl.multiple_of(PAD + me * rows, 16), rows)
    own = [pltpu.make_async_copy(
        pairs.at[:, pl.ds(pl.multiple_of(me * pw, 128), pw)], praw.at[own_rows, :], lsem.at[0])]
    for g in range(groups):
        own.append(pltpu.make_async_copy(
            inner.at[:, pl.ds(pl.multiple_of(me * width + g * gw, 128), gw)],
            xraw.at[g, own_rows, :], lsem.at[1 + g]))
    for c in own:
        c.start()

    @pl.when(ctx == 0)
    def _():
        praw[0:PAD, :] = jnp.zeros((PAD, pw), BF)
        for g in range(groups):
            xraw[g, 0:PAD, :] = jnp.zeros((PAD, gw), BF)

    v = step_raw[...].astype(F32) + step_bias[...]
    step = jnp.maximum(v, 0.0) + jnp.log1p(jnp.exp(-jnp.abs(v)))
    tri_r = lax.broadcasted_iota(jnp.int32, (BLOCK, BLOCK), 0)
    tri_c = lax.broadcasted_iota(jnp.int32, (BLOCK, BLOCK), 1)
    lower = tri_r >= tri_c
    lc = jnp.dot(lower.astype(F32), -jnp.exp(rate_log[...]) * step,
                 precision=lax.Precision.HIGHEST, preferred_element_type=F32)
    shifted = lc - jnp.log(step)
    shifted_t = shifted.T
    tail = jnp.exp(lc[BLOCK - 1 : BLOCK, :] - shifted)
    grow = jnp.exp(lc)

    def spread(cols, a):
        left = lax.broadcasted_iota(jnp.int32, (cols.shape[0], 2 * hd), 1) < hd
        return jnp.where(left, cols[:, a : a + 1], cols[:, a + 1 : a + 2])

    def arrived(i, ref, waits, own_copy):
        for w in waits:
            w.wait_recv()
        own_copy.wait()

        @pl.when(ctx < nctx - 1)
        def _():
            halo(i, ref).start()

        @pl.when(ctx > 0)
        def _():
            halo(i, ref).wait_recv()

    for g in range(groups):
        for a in range(0, per, 2):
            ex[g, :, a * hd : (a + 2) * hd] = spread(grow, g * per + a)

    arrived(0, praw, [p_copy(k, to(k), source(k)) for k in range(1, n)], own[0])
    conv_rows(praw, pc, w_pairs, me * pw, pw, store_plain)
    bts = []
    for g in range(groups):
        bt = pc[:, 2 * g * st : (2 * g + 1) * st].astype(F32).T.astype(BF)
        bts.append(bt)
        raw_scores = jnp.dot(
            pc[:, (2 * g + 1) * st : (2 * g + 2) * st], bt, preferred_element_type=F32)
        scores[g] = jnp.where(lower, raw_scores, 0.0)

    def prepare(g):
        arrived(1 + g, xraw.at[g],
                [x_copy(g, k, to(k), source(k)) for k in range(1, n)], own[1 + g])
        conv_rows(xraw.at[g], xc.at[g], w_inner, me * width + g * gw, gw, store_plain)
        for p in range(pieces):
            parts = []
            for a in range(p * WIDE // hd, (p + 1) * WIDE // hd, 2):
                x = xc[g, :, a * hd : (a + 2) * hd].astype(F32)
                parts.append((x * spread(tail, g * per + a)).astype(BF))
            weighted = jnp.concatenate(parts, axis=1)
            local[g, p] = jnp.dot(bts[g], weighted, preferred_element_type=F32)

            @pl.when(ctx == 0)
            def _():
                cout[g, p] = local[g, p].astype(BF)
                if nctx > 1:
                    chain(g, p).start()

    half = BLOCK // 2

    def intra(g, a):
        x = xc[g, :, a * hd : (a + 2) * hd]
        top, low = [], []
        for b in (a, a + 1):
            h = g * per + b
            col = lc[:, h : h + 1]
            row = shifted_t[h : h + 1, :]
            w0 = scores[g, :half, :half] * jnp.exp(jnp.minimum(col[:half] - row[:, :half], 30.0))
            top.append(jnp.dot(w0.astype(BF), x[:half], preferred_element_type=F32))
            w1 = scores[g, half:, :] * jnp.exp(jnp.minimum(col[half:] - row, 30.0))
            low.append(jnp.dot(w1.astype(BF), x, preferred_element_type=F32))
        left = lax.broadcasted_iota(jnp.int32, (half, 2 * hd), 1) < hd
        gain = spread(skip_gain[...], g * per + a)
        xf = x.astype(F32) * gain
        mixed[g, :half, a * hd : (a + 2) * hd] = jnp.where(left, top[0], top[1]) + xf[:half]
        mixed[g, half:, a * hd : (a + 2) * hd] = jnp.where(left, low[0], low[1]) + xf[half:]

    def serve(g, p):
        cols = slice(p * WIDE, (p + 1) * WIDE)

        @pl.when(ctx > 0)
        def _():
            chain(g, p).wait_recv()
            held = cin[g, p]

            @pl.when(ctx < nctx - 1)
            def _():
                decay = ex[g, BLOCK - 1 : BLOCK, cols]
                cout[g, p] = (decay * held.astype(F32) + local[g, p]).astype(BF)
                chain(g, p).start()

            cmat = pc[:, (2 * g + 1) * st : (2 * g + 2) * st]
            carried = jnp.dot(cmat, held, preferred_element_type=F32)
            mixed[g, :, cols] = mixed[g, :, cols] + carried * ex[g, :, cols]

    def work(g):
        for p in range(pieces):
            for a in range(p * WIDE // hd, (p + 1) * WIDE // hd, 2):
                intra(g, a)
            serve(g, p)

    own_out = []

    def finish(g):
        for k in list(range(1, n)) + [0]:
            who = to(k)
            rs = pl.ds(pl.multiple_of(who * rows, rows), rows)
            ssq = jnp.zeros((rows, 1), F32)
            for p in range(pieces):
                cols = slice(p * WIDE, (p + 1) * WIDE)
                z = gate[rs, g * gw + p * WIDE : g * gw + (p + 1) * WIDE].astype(F32)
                gated = mixed[g, rs, cols] * silu(z)
                mixed[g, rs, cols] = gated
                ssq = ssq + jnp.sum(gated * gated, axis=1, keepdims=True)
            inv = lax.rsqrt(ssq / gw + 1e-05)
            for p in range(pieces):
                cols = slice(p * WIDE, (p + 1) * WIDE)
                gain = norm_gain[:, g * gw + p * WIDE : g * gw + (p + 1) * WIDE]
                outbuf[g, rs, cols] = (mixed[g, rs, cols] * inv * gain).astype(BF)
            if k:
                o_copy(g, k, who, me).start()
            else:
                c = pltpu.make_async_copy(
                    outbuf.at[g, rs, :],
                    out.at[:, pl.ds(pl.multiple_of(me * width + g * gw, 128), gw)], olsem.at[g])
                c.start()
                own_out.append(c)

    prepare(0)
    work(0)
    for g in range(1, groups):
        prepare(g)
        finish(g - 1)
        work(g)
    finish(groups - 1)

    for k in range(1, n):
        p_copy(k, to(k), me).wait_send()
        for g in range(groups):
            x_copy(g, k, to(k), me).wait_send()
            o_copy(g, k, to(k), me).wait_send()
            o_copy(g, k, to(k), source(k)).wait_recv()
    for c in own_out:
        c.wait()

    @pl.when(ctx < nctx - 1)
    def _():
        halo(0, praw).wait_send()
        for g in range(groups):
            halo(1 + g, xraw.at[g]).wait_send()
            for p in range(pieces):
                chain(g, p).wait_send()


def on_device(
    inner_raw, pairs_raw, gate_raw, step_raw, step_bias, rate_log,
    skip_gain, conv_inner, conv_pairs, norm_gain,
):
    n = lax.axis_size("head")
    nctx = lax.axis_size("context")
    rows, full = inner_raw.shape
    width = gate_raw.shape[1]
    heads = step_raw.shape[1]
    groups = pairs_raw.shape[1] // n
    st = pairs_raw.shape[3]
    pw = groups * 2 * st
    gw = width // groups
    pieces = gw // WIDE
    pairs = pairs_raw.reshape(rows, -1)
    w_pairs = conv_pairs.reshape(conv_pairs.shape[0], -1)
    vm = pl.BlockSpec(memory_space=pltpu.VMEM)
    hbm = pl.BlockSpec(memory_space=pl.ANY)
    dma = pltpu.SemaphoreType.DMA
    return pl.pallas_call(
        functools.partial(kernel, n, nctx, groups, heads),
        out_shape=jax.ShapeDtypeStruct((rows, full), BF),
        in_specs=[hbm, hbm] + [vm] * 8,
        out_specs=hbm,
        scratch_shapes=[
            pltpu.VMEM((groups, PAD + BLOCK, gw), BF),
            pltpu.VMEM((PAD + BLOCK, pw), BF),
            pltpu.VMEM((groups, BLOCK, gw), BF),
            pltpu.VMEM((BLOCK, pw), BF),
            pltpu.VMEM((groups, BLOCK, gw), F32),
            pltpu.VMEM((groups, BLOCK, gw), F32),
            pltpu.VMEM((groups, pieces, st, WIDE), F32),
            pltpu.VMEM((groups, BLOCK, BLOCK), F32),
            pltpu.VMEM((groups, pieces, st, WIDE), BF),
            pltpu.VMEM((groups, pieces, st, WIDE), BF),
            pltpu.VMEM((groups, BLOCK, gw), BF),
            dma((groups, n - 1)), dma((groups, n - 1)),
            dma((n - 1,)), dma((n - 1,)),
            dma((1 + groups,)),
            dma((1 + groups,)), dma((1 + groups,)),
            dma((groups, pieces)), dma((groups, pieces)),
            dma((groups, n - 1)), dma((groups, n - 1)),
            dma((groups,)),
        ],
        compiler_params=pltpu.CompilerParams(
            collective_id=0, has_side_effects=True, vmem_limit_bytes=40 * 1024 * 1024),
        cost_estimate=pl.CostEstimate(
            flops=700_000_000, bytes_accessed=4_000_000, transcendentals=4_000_000),
        name="mixer",
    )(
        inner_raw, pairs, gate_raw, step_raw, step_bias[None, :], rate_log[None, :],
        skip_gain[None, :], conv_inner, w_pairs, norm_gain[None, :],
    )


def solution(mesh):
    placed = (
        P(("rollout", "context", "head"), None),
        P(("rollout", "context", "head"), None, None, None),
        P(("rollout", "context"), "head"),
        P(("rollout", "context"), "head"),
        P("head"),
        P("head"),
        P("head"),
        P(),
        P(),
        P("head"),
    )
    return jax.shard_map(
        on_device,
        mesh=mesh,
        in_specs=placed,
        out_specs=P(("rollout", "context", "head"), None),
        check_vma=False,
    )
```

```python
import functools

import jax
import jax.numpy as jnp
from jax import lax
from jax.experimental import pallas as pl
from jax.experimental.pallas import tpu as pltpu
from jax.sharding import PartitionSpec as P

BLOCK = 256
PAD = 16
CHUNK = 32
WIDE = 256
PIECE = 512
BF = jnp.bfloat16
F32 = jnp.float32


def silu(v):
    return v / (1.0 + jnp.exp(-v))


def conv_rows(src, dst, weight, first_col, cols, dst_of):
    rows = src.shape[0] - PAD
    taps = weight.shape[0] - 1

    def step(i, carry):
        r0 = pl.multiple_of(i * CHUNK, CHUNK)
        for c0 in range(0, cols, WIDE):
            raw = src[pl.ds(r0, CHUNK + PAD), c0 : c0 + WIDE].astype(F32)
            w = weight[:, pl.ds(pl.multiple_of(first_col + c0, WIDE), WIDE)]
            total = w[taps : taps + 1]
            for k in range(taps):
                o = PAD - taps + k
                total = total + w[k : k + 1] * raw[o : o + CHUNK]
            dst_of(dst, r0, c0, silu(total).astype(BF))
        return carry

    lax.fori_loop(0, rows // CHUNK, step, 0)


def store_plain(dst, r0, c0, value):
    dst[pl.ds(r0, CHUNK), c0 : c0 + WIDE] = value


def kernel(
    n, nctx, groups, heads_local,
    inner, pairs, gate_hbm, step_raw, step_bias, rate_log, skip_gain, w_inner, w_pairs, norm_gain,
    out,
    gbuf, xraw, praw, xc, pc, mixed, ex, local, scores, cin, cout, outbuf,
    xs, xr, ps, pr, lsem, hs, hr, cs, cr, os, orr, olsem, gsem,
):
    me = lax.axis_index("head")
    ctx = lax.axis_index("context")
    rows = inner.shape[0]
    width = gate_hbm.shape[1]
    gate = gbuf
    gw = width // groups
    per = heads_local // groups
    hd = width // heads_local
    pw = praw.shape[1]
    st = pw // (2 * groups)
    pieces = gw // WIDE
    count = width // PIECE

    gate_copy = pltpu.make_async_copy(gate_hbm, gbuf, gsem)
    gate_copy.start()

    barrier = pltpu.get_barrier_semaphore()
    for k in range(1, n):
        pl.semaphore_signal(barrier, inc=1, device_id={"head": lax.rem(me + k, n)})

    @pl.when(ctx > 0)
    def _():
        pl.semaphore_signal(barrier, inc=1, device_id={"context": ctx - 1})

    @pl.when(ctx < nctx - 1)
    def _():
        pl.semaphore_signal(barrier, inc=1, device_id={"context": ctx + 1})

    links = jnp.where(ctx > 0, 1, 0) + jnp.where(ctx < nctx - 1, 1, 0)
    pl.semaphore_wait(barrier, n - 1 + links)

    def p_copy(k, who, at):
        return pltpu.make_async_remote_copy(
            src_ref=pairs.at[:, pl.ds(pl.multiple_of(who * pw, 128), pw)],
            dst_ref=praw.at[pl.ds(pl.multiple_of(PAD + at * rows, 16), rows), :],
            send_sem=ps.at[k - 1], recv_sem=pr.at[k - 1], device_id={"head": who})

    def x_copy(q, k, who, at):
        return pltpu.make_async_remote_copy(
            src_ref=inner.at[:, pl.ds(pl.multiple_of(who * width + q * PIECE, 128), PIECE)],
            dst_ref=xraw.at[q, pl.ds(pl.multiple_of(PAD + at * rows, 16), rows), :],
            send_sem=xs.at[q, k - 1], recv_sem=xr.at[q, k - 1], device_id={"head": who})

    def o_copy(g, k, who, at):
        return pltpu.make_async_remote_copy(
            src_ref=outbuf.at[g, pl.ds(pl.multiple_of(who * rows, 16), rows), :],
            dst_ref=out.at[:, pl.ds(pl.multiple_of(at * width + g * gw, 128), gw)],
            send_sem=os.at[g, k - 1], recv_sem=orr.at[g, k - 1], device_id={"head": who})

    def halo(i, ref):
        last = ref.shape[0] - PAD
        return pltpu.make_async_remote_copy(
            src_ref=ref.at[last:, :], dst_ref=ref.at[0:PAD, :],
            send_sem=hs.at[i], recv_sem=hr.at[i],
            device_id={"context": lax.rem(ctx + 1, nctx)})

    def chain(g, p):
        return pltpu.make_async_remote_copy(
            src_ref=cout.at[g, p], dst_ref=cin.at[g, p],
            send_sem=cs.at[g, p], recv_sem=cr.at[g, p],
            device_id={"context": lax.rem(ctx + 1, nctx)})

    def to(k):
        return lax.rem(me + k, n)

    def source(k):
        return lax.rem(me + n - k, n)

    for k in range(1, n):
        p_copy(k, to(k), me).start()
    for q in range(count):
        for k in range(1, n):
            x_copy(q, k, to(k), me).start()
    own_rows = pl.ds(pl.multiple_of(PAD + me * rows, 16), rows)
    own = [pltpu.make_async_copy(
        pairs.at[:, pl.ds(pl.multiple_of(me * pw, 128), pw)], praw.at[own_rows, :], lsem.at[0])]
    for q in range(count):
        own.append(pltpu.make_async_copy(
            inner.at[:, pl.ds(pl.multiple_of(me * width + q * PIECE, 128), PIECE)],
            xraw.at[q, own_rows, :], lsem.at[1 + q]))
    for c in own:
        c.start()

    @pl.when(ctx == 0)
    def _():
        praw[0:PAD, :] = jnp.zeros((PAD, pw), BF)
        for q in range(count):
            xraw[q, 0:PAD, :] = jnp.zeros((PAD, PIECE), BF)

    v = step_raw[...].astype(F32) + step_bias[...].T
    step = jnp.maximum(v, 0.0) + jnp.log1p(jnp.exp(-jnp.abs(v)))
    tri_r = lax.broadcasted_iota(jnp.int32, (BLOCK, BLOCK), 0)
    tri_c = lax.broadcasted_iota(jnp.int32, (BLOCK, BLOCK), 1)
    lower = tri_r >= tri_c
    lc_t = jnp.dot(-jnp.exp(rate_log[...].T) * step, (tri_r <= tri_c).astype(F32),
                   precision=lax.Precision.HIGHEST, preferred_element_type=F32)
    shifted_t = lc_t - jnp.log(step)
    lc = lc_t.T
    shifted = shifted_t.T
    tail = jnp.exp(lc[BLOCK - 1 : BLOCK, :] - shifted)
    grow = jnp.exp(lc)

    def spread(cols, a):
        left = lax.broadcasted_iota(jnp.int32, (cols.shape[0], 2 * hd), 1) < hd
        return jnp.where(left, cols[:, a : a + 1], cols[:, a + 1 : a + 2])

    def arrived(i, ref, waits, own_copy):
        for w in waits:
            w.wait_recv()
        own_copy.wait()

        @pl.when(ctx < nctx - 1)
        def _():
            halo(i, ref).start()

        @pl.when(ctx > 0)
        def _():
            halo(i, ref).wait_recv()

    for g in range(groups):
        for a in range(0, per, 2):
            ex[g, :, a * hd : (a + 2) * hd] = spread(grow, g * per + a)

    arrived(0, praw, [p_copy(k, to(k), source(k)) for k in range(1, n)], own[0])
    conv_rows(praw, pc, w_pairs, me * pw, pw, store_plain)
    bts = []
    for g in range(groups):
        bt = pc[:, 2 * g * st : (2 * g + 1) * st].astype(F32).T.astype(BF)
        bts.append(bt)
        raw_scores = jnp.dot(
            pc[:, (2 * g + 1) * st : (2 * g + 2) * st], bt, preferred_element_type=F32)
        scores[g] = jnp.where(lower, raw_scores, 0.0)

    def prepare(q):
        arrived(1 + q, xraw.at[q],
                [x_copy(q, k, to(k), source(k)) for k in range(1, n)], own[1 + q])
        conv_rows(xraw.at[q], xc.at[q], w_inner, me * width + q * PIECE, PIECE, store_plain)
        for c0 in range(0, PIECE, WIDE):
            g, first = divmod(q * PIECE + c0, gw)
            p = first // WIDE
            parts = []
            for o in range(c0, c0 + WIDE, 2 * hd):
                x = xc[q, :, o : o + 2 * hd].astype(F32)
                parts.append((x * spread(tail, (q * PIECE + o) // hd)).astype(BF))
            weighted = jnp.concatenate(parts, axis=1)
            state = jnp.dot(bts[g], weighted, preferred_element_type=F32)
            local[g, p] = state

            @pl.when(ctx == 0)
            def _():
                cout[g, p] = state.astype(BF)
                if nctx > 1:
                    chain(g, p).start()

    half = BLOCK // 2

    def intra(g, a):
        q, o = divmod(g * gw + a * hd, PIECE)
        x = xc[q, :, o : o + 2 * hd]
        top, low = [], []
        for b in (a, a + 1):
            h = g * per + b
            col = lc[:, h : h + 1]
            row = shifted_t[h : h + 1, :]
            w0 = scores[g, :half, :half] * jnp.exp(jnp.minimum(col[:half] - row[:, :half], 30.0))
            top.append(jnp.dot(w0.astype(BF), x[:half], preferred_element_type=F32))
            w1 = scores[g, half:, :] * jnp.exp(jnp.minimum(col[half:] - row, 30.0))
            low.append(jnp.dot(w1.astype(BF), x, preferred_element_type=F32))
        left = lax.broadcasted_iota(jnp.int32, (half, 2 * hd), 1) < hd
        gain = spread(skip_gain[...], g * per + a)
        xf = x.astype(F32) * gain
        mixed[g, :half, a * hd : (a + 2) * hd] = jnp.where(left, top[0], top[1]) + xf[:half]
        mixed[g, half:, a * hd : (a + 2) * hd] = jnp.where(left, low[0], low[1]) + xf[half:]

    def forward(g, p):
        @pl.when(jnp.logical_and(ctx > 0, ctx < nctx - 1))
        def _():
            chain(g, p).wait_recv()
            decay = ex[g, BLOCK - 1 : BLOCK, p * WIDE : (p + 1) * WIDE]
            cout[g, p] = (decay * cin[g, p].astype(F32) + local[g, p]).astype(BF)
            chain(g, p).start()

    def absorb(g):
        @pl.when(ctx > 0)
        def _():
            for p in range(pieces):
                cols = slice(p * WIDE, (p + 1) * WIDE)

                @pl.when(ctx == nctx - 1)
                def _():
                    chain(g, p).wait_recv()

                cmat = pc[:, (2 * g + 1) * st : (2 * g + 2) * st]
                carried = jnp.dot(cmat, cin[g, p], preferred_element_type=F32)
                mixed[g, :, cols] = mixed[g, :, cols] + carried * ex[g, :, cols]

    own_out = []

    def finish(g):
        for k in list(range(1, n)) + [0]:
            who = to(k)
            rs = pl.ds(pl.multiple_of(who * rows, rows), rows)
            ssq = jnp.zeros((rows, 1), F32)
            for p in range(pieces):
                cols = slice(p * WIDE, (p + 1) * WIDE)
                z = gate[rs, g * gw + p * WIDE : g * gw + (p + 1) * WIDE].astype(F32)
                gated = mixed[g, rs, cols] * silu(z)
                mixed[g, rs, cols] = gated
                ssq = ssq + jnp.sum(gated * gated, axis=1, keepdims=True)
            inv = lax.rsqrt(ssq / gw + 1e-05)
            for p in range(pieces):
                cols = slice(p * WIDE, (p + 1) * WIDE)
                gain = norm_gain[:, g * gw + p * WIDE : g * gw + (p + 1) * WIDE]
                outbuf[g, rs, cols] = (mixed[g, rs, cols] * inv * gain).astype(BF)
            if k:
                o_copy(g, k, who, me).start()
            else:
                c = pltpu.make_async_copy(
                    outbuf.at[g, rs, :],
                    out.at[:, pl.ds(pl.multiple_of(me * width + g * gw, 128), gw)], olsem.at[g])
                c.start()
                own_out.append(c)

    for q in range(count):
        prepare(q)
        for c0 in range(q * PIECE, (q + 1) * PIECE, WIDE):
            g, first = divmod(c0, gw)
            for a in range(first // hd, (first + WIDE) // hd, 2):
                intra(g, a)
            forward(g, first // WIDE)
    gate_copy.wait()
    for g in range(groups):
        absorb(g)
        finish(g)

    for k in range(1, n):
        p_copy(k, to(k), me).wait_send()
        for q in range(count):
            x_copy(q, k, to(k), me).wait_send()
        for g in range(groups):
            o_copy(g, k, to(k), me).wait_send()
            o_copy(g, k, to(k), source(k)).wait_recv()
    for c in own_out:
        c.wait()

    @pl.when(ctx < nctx - 1)
    def _():
        halo(0, praw).wait_send()
        for q in range(count):
            halo(1 + q, xraw.at[q]).wait_send()
        for g in range(groups):
            for p in range(pieces):
                chain(g, p).wait_send()


def on_device(
    inner_raw, pairs_raw, gate_raw, step_raw, step_bias, rate_log,
    skip_gain, conv_inner, conv_pairs, norm_gain,
):
    n = lax.axis_size("head")
    nctx = lax.axis_size("context")
    rows, full = inner_raw.shape
    width = gate_raw.shape[1]
    heads = step_raw.shape[1]
    groups = pairs_raw.shape[1] // n
    st = pairs_raw.shape[3]
    pw = groups * 2 * st
    gw = width // groups
    pieces = gw // WIDE
    count = width // PIECE
    pairs = pairs_raw.reshape(rows, -1)
    w_pairs = conv_pairs.reshape(conv_pairs.shape[0], -1)
    vm = pl.BlockSpec(memory_space=pltpu.VMEM)
    hbm = pl.BlockSpec(memory_space=pl.ANY)
    far = pl.BlockSpec(memory_space=pltpu.MemorySpace.HBM)
    dma = pltpu.SemaphoreType.DMA
    return pl.pallas_call(
        functools.partial(kernel, n, nctx, groups, heads),
        out_shape=jax.ShapeDtypeStruct((rows, full), BF),
        in_specs=[far, hbm, far] + [vm] * 7,
        out_specs=hbm,
        scratch_shapes=[
            pltpu.VMEM((BLOCK, width), BF),
            pltpu.VMEM((count, PAD + BLOCK, PIECE), BF),
            pltpu.VMEM((PAD + BLOCK, pw), BF),
            pltpu.VMEM((count, BLOCK, PIECE), BF),
            pltpu.VMEM((BLOCK, pw), BF),
            pltpu.VMEM((groups, BLOCK, gw), F32),
            pltpu.VMEM((groups, BLOCK, gw), F32),
            pltpu.VMEM((groups, pieces, st, WIDE), F32),
            pltpu.VMEM((groups, BLOCK, BLOCK), F32),
            pltpu.VMEM((groups, pieces, st, WIDE), BF),
            pltpu.VMEM((groups, pieces, st, WIDE), BF),
            pltpu.VMEM((groups, BLOCK, gw), BF),
            dma((count, n - 1)), dma((count, n - 1)),
            dma((n - 1,)), dma((n - 1,)),
            dma((1 + count,)),
            dma((1 + count,)), dma((1 + count,)),
            dma((groups, pieces)), dma((groups, pieces)),
            dma((groups, n - 1)), dma((groups, n - 1)),
            dma((groups,)),
            dma,
        ],
        compiler_params=pltpu.CompilerParams(
            collective_id=0, has_side_effects=True, vmem_limit_bytes=40 * 1024 * 1024),
        cost_estimate=pl.CostEstimate(
            flops=700_000_000, bytes_accessed=4_000_000, transcendentals=4_000_000),
        name="mixer",
    )(
        inner_raw, pairs, gate_raw, step_raw.T, step_bias[None, :], rate_log[None, :],
        skip_gain[None, :], conv_inner, w_pairs, norm_gain[None, :],
    )


def solution(mesh):
    placed = (
        P(("rollout", "context", "head"), None),
        P(("rollout", "context", "head"), None, None, None),
        P(("rollout", "context"), "head"),
        P(("rollout", "context"), "head"),
        P("head"),
        P("head"),
        P("head"),
        P(),
        P(),
        P("head"),
    )
    return jax.shard_map(
        on_device,
        mesh=mesh,
        in_specs=placed,
        out_specs=P(("rollout", "context", "head"), None),
        check_vma=False,
    )
```

```python
import functools

import jax
import jax.numpy as jnp
from jax import lax
from jax.experimental import pallas as pl
from jax.experimental.pallas import tpu as pltpu
from jax.sharding import PartitionSpec as P

BLOCK = 256
PAD = 16
CHUNK = 32
WIDE = 256
LOG2E = 1.4426950408889634
PIECE = 512
BF = jnp.bfloat16
F32 = jnp.float32


def silu(v):
    half = 0.5 * v
    return half + half * jnp.tanh(half)


def conv_rows(src, dst, weight_of, taps, cols, wide):
    rows = src.shape[0] - PAD

    def step(i, carry):
        r0 = pl.multiple_of(i * CHUNK, CHUNK)
        for c0 in range(0, cols, wide):
            raw = src[pl.ds(r0, CHUNK + PAD), c0 : c0 + wide].astype(F32)
            w = weight_of(c0)
            total = w[taps]
            for k in range(taps):
                o = PAD - taps + k
                total = total + w[k] * raw[o : o + CHUNK]
            dst[pl.ds(r0, CHUNK), c0 : c0 + wide] = silu(total).astype(BF)
        return carry

    lax.fori_loop(0, rows // CHUNK, step, 0)


def kernel(
    n, nctx, groups, heads_local,
    inner, pairs, gate_hbm, step_raw, step_bias, rate_log, skip_gain, w_inner, w_pairs, norm_gain,
    out,
    gbuf, act, xraw, praw, xc, pc, mixed, ex, local, scores, cin, cout, outbuf,
    xs, xr, ps, pr, lsem, hs, hr, cs, cr, os, orr, olsem, gsem,
):
    me = lax.axis_index("head")
    ctx = lax.axis_index("context")
    rows = inner.shape[0]
    width = gate_hbm.shape[1]
    gate = gbuf
    gw = width // groups
    per = heads_local // groups
    hd = width // heads_local
    pw = praw.shape[1]
    st = pw // (2 * groups)
    pieces = gw // WIDE
    count = width // PIECE

    gate_copy = pltpu.make_async_copy(gate_hbm, gbuf, gsem)
    gate_copy.start()

    barrier = pltpu.get_barrier_semaphore()
    for k in range(1, n):
        pl.semaphore_signal(barrier, inc=1, device_id={"head": lax.rem(me + k, n)})

    @pl.when(ctx > 0)
    def _():
        pl.semaphore_signal(barrier, inc=1, device_id={"context": ctx - 1})

    @pl.when(ctx < nctx - 1)
    def _():
        pl.semaphore_signal(barrier, inc=1, device_id={"context": ctx + 1})

    links = jnp.where(ctx > 0, 1, 0) + jnp.where(ctx < nctx - 1, 1, 0)
    pl.semaphore_wait(barrier, n - 1 + links)

    def p_copy(k, who, at):
        return pltpu.make_async_remote_copy(
            src_ref=pairs.at[:, pl.ds(pl.multiple_of(who * pw, 128), pw)],
            dst_ref=praw.at[pl.ds(pl.multiple_of(PAD + at * rows, 16), rows), :],
            send_sem=ps.at[k - 1], recv_sem=pr.at[k - 1], device_id={"head": who})

    def x_copy(q, k, who, at):
        return pltpu.make_async_remote_copy(
            src_ref=inner.at[:, pl.ds(pl.multiple_of(who * width + q * PIECE, 128), PIECE)],
            dst_ref=xraw.at[q, pl.ds(pl.multiple_of(PAD + at * rows, 16), rows), :],
            send_sem=xs.at[q, k - 1], recv_sem=xr.at[q, k - 1], device_id={"head": who})

    def o_copy(g, k, who, at):
        return pltpu.make_async_remote_copy(
            src_ref=outbuf.at[g, pl.ds(pl.multiple_of(who * rows, 16), rows), :],
            dst_ref=out.at[:, pl.ds(pl.multiple_of(at * width + g * gw, 128), gw)],
            send_sem=os.at[g, k - 1], recv_sem=orr.at[g, k - 1], device_id={"head": who})

    def halo(i, ref):
        last = ref.shape[0] - PAD
        return pltpu.make_async_remote_copy(
            src_ref=ref.at[last:, :], dst_ref=ref.at[0:PAD, :],
            send_sem=hs.at[i], recv_sem=hr.at[i],
            device_id={"context": lax.rem(ctx + 1, nctx)})

    def chain(g, p):
        return pltpu.make_async_remote_copy(
            src_ref=cout.at[g, p], dst_ref=cin.at[g, p],
            send_sem=cs.at[g, p], recv_sem=cr.at[g, p],
            device_id={"context": lax.rem(ctx + 1, nctx)})

    def to(k):
        return lax.rem(me + k, n)

    def source(k):
        return lax.rem(me + n - k, n)

    for k in range(1, n):
        p_copy(k, to(k), me).start()
    for q in range(count):
        for k in range(1, n):
            x_copy(q, k, to(k), me).start()
    own_rows = pl.ds(pl.multiple_of(PAD + me * rows, 16), rows)
    own = [pltpu.make_async_copy(
        pairs.at[:, pl.ds(pl.multiple_of(me * pw, 128), pw)], praw.at[own_rows, :], lsem.at[0])]
    for q in range(count):
        own.append(pltpu.make_async_copy(
            inner.at[:, pl.ds(pl.multiple_of(me * width + q * PIECE, 128), PIECE)],
            xraw.at[q, own_rows, :], lsem.at[1 + q]))
    for c in own:
        c.start()

    @pl.when(ctx == 0)
    def _():
        praw[0:PAD, :] = jnp.zeros((PAD, pw), BF)
        for q in range(count):
            xraw[q, 0:PAD, :] = jnp.zeros((PAD, PIECE), BF)

    v = step_raw[...].astype(F32) + step_bias[...].T
    step = jnp.maximum(v, 0.0) + jnp.log1p(jnp.exp(-jnp.abs(v)))
    tri_r = lax.broadcasted_iota(jnp.int32, (BLOCK, BLOCK), 0)
    tri_c = lax.broadcasted_iota(jnp.int32, (BLOCK, BLOCK), 1)
    lower = tri_r >= tri_c
    lc_t = jnp.dot(-jnp.exp(rate_log[...].T) * step, (tri_r <= tri_c).astype(F32),
                   precision=lax.Precision.HIGHEST, preferred_element_type=F32)
    shifted_t = lc_t - jnp.log(step)
    lc = lc_t.T
    shifted = shifted_t.T
    tail = jnp.exp(lc[BLOCK - 1 : BLOCK, :] - shifted)
    grow = jnp.exp(lc)

    lc2 = lc * LOG2E
    shifted2_t = shifted_t * LOG2E

    def spread(cols, a):
        left = lax.broadcasted_iota(jnp.int32, (cols.shape[0], 2 * hd), 1) < hd
        return jnp.where(left, cols[:, a : a + 1], cols[:, a + 1 : a + 2])

    def arrived(i, ref, waits, own_copy):
        for w in waits:
            w.wait_recv()
        own_copy.wait()

        @pl.when(ctx < nctx - 1)
        def _():
            halo(i, ref).start()

        @pl.when(ctx > 0)
        def _():
            halo(i, ref).wait_recv()

    for g in range(groups):
        for a in range(0, per, 2):
            ex[g, :, a * hd : (a + 2) * hd] = spread(grow, g * per + a)

    gate_copy.wait()

    def open_gate(i, carry):
        at = pl.ds(pl.multiple_of(i * CHUNK, CHUNK), CHUNK)
        for c0 in range(0, width, WIDE):
            act[at, c0 : c0 + WIDE] = silu(gate[at, c0 : c0 + WIDE].astype(F32))
        return carry

    lax.fori_loop(0, BLOCK // CHUNK, open_gate, 0)
    arrived(0, praw, [p_copy(k, to(k), source(k)) for k in range(1, n)], own[0])
    taps = w_inner.shape[0] - 1

    def pair_weight(c0):
        g, b = divmod(c0 // st, 2)
        return [w_pairs[k, me * groups + g, b : b + 1, :] for k in range(taps + 1)]

    def inner_weight(q):
        def rows_at(c0):
            at = pl.ds(pl.multiple_of(me * width + q * PIECE + c0, WIDE), WIDE)
            return [w_inner[k : k + 1, at] for k in range(taps + 1)]

        return rows_at

    conv_rows(praw, pc, pair_weight, taps, pw, st)
    bts = []
    for g in range(groups):
        bt = pc[:, 2 * g * st : (2 * g + 1) * st].astype(F32).T.astype(BF)
        bts.append(bt)
        raw_scores = jnp.dot(
            pc[:, (2 * g + 1) * st : (2 * g + 2) * st], bt, preferred_element_type=F32)
        scores[g] = jnp.where(lower, raw_scores, 0.0)

    def prepare(q):
        arrived(1 + q, xraw.at[q],
                [x_copy(q, k, to(k), source(k)) for k in range(1, n)], own[1 + q])
        conv_rows(xraw.at[q], xc.at[q], inner_weight(q), taps, PIECE, WIDE)
        for c0 in range(0, PIECE, WIDE):
            g, first = divmod(q * PIECE + c0, gw)
            p = first // WIDE
            parts = []
            for o in range(c0, c0 + WIDE, 2 * hd):
                x = xc[q, :, o : o + 2 * hd].astype(F32)
                parts.append((x * spread(tail, (q * PIECE + o) // hd)).astype(BF))
            weighted = jnp.concatenate(parts, axis=1)
            state = jnp.dot(bts[g], weighted, preferred_element_type=F32)
            local[g, p] = state

            @pl.when(ctx == 0)
            def _():
                cout[g, p] = state.astype(BF)
                if nctx > 1:
                    chain(g, p).start()

    half = BLOCK // 2

    def intra(g, a):
        q, o = divmod(g * gw + a * hd, PIECE)
        x = xc[q, :, o : o + 2 * hd]
        top, low = [], []
        for b in (a, a + 1):
            h = g * per + b
            col = lc2[:, h : h + 1]
            row = shifted2_t[h : h + 1, :]
            w0 = scores[g, :half, :half] * jnp.exp2(jnp.minimum(col[:half] - row[:, :half], 40.0))
            top.append(jnp.dot(w0.astype(BF), x[:half], preferred_element_type=F32))
            w1 = scores[g, half:, :half] * jnp.exp2(col[half:] - row[:, :half])
            w2 = scores[g, half:, half:] * jnp.exp2(jnp.minimum(col[half:] - row[:, half:], 40.0))
            w = jnp.concatenate([w1.astype(BF), w2.astype(BF)], axis=1)
            low.append(jnp.dot(w, x, preferred_element_type=F32))
        left = lax.broadcasted_iota(jnp.int32, (half, 2 * hd), 1) < hd
        gain = spread(skip_gain[...], g * per + a)
        xf = x.astype(F32) * gain
        mixed[g, :half, a * hd : (a + 2) * hd] = jnp.where(left, top[0], top[1]) + xf[:half]
        mixed[g, half:, a * hd : (a + 2) * hd] = jnp.where(left, low[0], low[1]) + xf[half:]

    def forward(g, p):
        @pl.when(jnp.logical_and(ctx > 0, ctx < nctx - 1))
        def _():
            chain(g, p).wait_recv()
            decay = ex[g, BLOCK - 1 : BLOCK, p * WIDE : (p + 1) * WIDE]
            cout[g, p] = (decay * cin[g, p].astype(F32) + local[g, p]).astype(BF)
            chain(g, p).start()

    def absorb(g):
        @pl.when(ctx > 0)
        def _():
            for p in range(pieces):
                cols = slice(p * WIDE, (p + 1) * WIDE)

                @pl.when(ctx == nctx - 1)
                def _():
                    chain(g, p).wait_recv()

                cmat = pc[:, (2 * g + 1) * st : (2 * g + 2) * st]
                carried = jnp.dot(cmat, cin[g, p], preferred_element_type=F32)
                mixed[g, :, cols] = mixed[g, :, cols] + carried * ex[g, :, cols]

    own_out = []

    def finish(g):
        for k in list(range(1, n)) + [0]:
            who = to(k)
            rs = pl.ds(pl.multiple_of(who * rows, rows), rows)
            ssq = jnp.zeros((rows, 1), F32)
            for p in range(pieces):
                cols = slice(p * WIDE, (p + 1) * WIDE)
                z = act[rs, g * gw + p * WIDE : g * gw + (p + 1) * WIDE]
                gated = mixed[g, rs, cols] * z
                mixed[g, rs, cols] = gated
                ssq = ssq + jnp.sum(gated * gated, axis=1, keepdims=True)
            inv = lax.rsqrt(ssq / gw + 1e-05)
            for p in range(pieces):
                cols = slice(p * WIDE, (p + 1) * WIDE)
                gain = norm_gain[:, g * gw + p * WIDE : g * gw + (p + 1) * WIDE]
                outbuf[g, rs, cols] = (mixed[g, rs, cols] * inv * gain).astype(BF)
            if k:
                o_copy(g, k, who, me).start()
            else:
                c = pltpu.make_async_copy(
                    outbuf.at[g, rs, :],
                    out.at[:, pl.ds(pl.multiple_of(me * width + g * gw, 128), gw)], olsem.at[g])
                c.start()
                own_out.append(c)

    def pieces_of(q):
        return [divmod(c0, gw) for c0 in range(q * PIECE, (q + 1) * PIECE, WIDE)]

    def intra_piece(q):
        for g, first in pieces_of(q):
            for a in range(first // hd, (first + WIDE) // hd, 2):
                intra(g, a)

    def forward_piece(q):
        for g, first in pieces_of(q):
            forward(g, first // WIDE)

    prepare(0)
    intra_piece(0)
    for q in range(1, count):
        prepare(q)
        forward_piece(q - 1)
    per_group = gw // PIECE
    for q in range(1, count):
        intra_piece(q)
        if q == 1:
            forward_piece(count - 1)
        if q % per_group == per_group - 1:
            absorb(q // per_group)
            finish(q // per_group)

    for k in range(1, n):
        p_copy(k, to(k), me).wait_send()
        for q in range(count):
            x_copy(q, k, to(k), me).wait_send()
        for g in range(groups):
            o_copy(g, k, to(k), me).wait_send()
            o_copy(g, k, to(k), source(k)).wait_recv()
    for c in own_out:
        c.wait()

    @pl.when(ctx < nctx - 1)
    def _():
        halo(0, praw).wait_send()
        for q in range(count):
            halo(1 + q, xraw.at[q]).wait_send()
        for g in range(groups):
            for p in range(pieces):
                chain(g, p).wait_send()


def on_device(
    inner_raw, pairs_raw, gate_raw, step_raw, step_bias, rate_log,
    skip_gain, conv_inner, conv_pairs, norm_gain,
):
    n = lax.axis_size("head")
    nctx = lax.axis_size("context")
    rows, full = inner_raw.shape
    width = gate_raw.shape[1]
    heads = step_raw.shape[1]
    groups = pairs_raw.shape[1] // n
    st = pairs_raw.shape[3]
    pw = groups * 2 * st
    gw = width // groups
    pieces = gw // WIDE
    count = width // PIECE
    pairs = pairs_raw.reshape(rows, -1)
    vm = pl.BlockSpec(memory_space=pltpu.VMEM)
    hbm = pl.BlockSpec(memory_space=pl.ANY)
    far = pl.BlockSpec(memory_space=pltpu.MemorySpace.HBM)
    dma = pltpu.SemaphoreType.DMA
    return pl.pallas_call(
        functools.partial(kernel, n, nctx, groups, heads),
        out_shape=jax.ShapeDtypeStruct((rows, full), BF),
        in_specs=[far, hbm, far] + [vm] * 7,
        out_specs=hbm,
        scratch_shapes=[
            pltpu.VMEM((BLOCK, width), BF),
            pltpu.VMEM((BLOCK, width), F32),
            pltpu.VMEM((count, PAD + BLOCK, PIECE), BF),
            pltpu.VMEM((PAD + BLOCK, pw), BF),
            pltpu.VMEM((count, BLOCK, PIECE), BF),
            pltpu.VMEM((BLOCK, pw), BF),
            pltpu.VMEM((groups, BLOCK, gw), F32),
            pltpu.VMEM((groups, BLOCK, gw), F32),
            pltpu.VMEM((groups, pieces, st, WIDE), F32),
            pltpu.VMEM((groups, BLOCK, BLOCK), F32),
            pltpu.VMEM((groups, pieces, st, WIDE), BF),
            pltpu.VMEM((groups, pieces, st, WIDE), BF),
            pltpu.VMEM((groups, BLOCK, gw), BF),
            dma((count, n - 1)), dma((count, n - 1)),
            dma((n - 1,)), dma((n - 1,)),
            dma((1 + count,)),
            dma((1 + count,)), dma((1 + count,)),
            dma((groups, pieces)), dma((groups, pieces)),
            dma((groups, n - 1)), dma((groups, n - 1)),
            dma((groups,)),
            dma,
        ],
        compiler_params=pltpu.CompilerParams(
            collective_id=0, has_side_effects=True, vmem_limit_bytes=58 * 1024 * 1024),
        cost_estimate=pl.CostEstimate(
            flops=700_000_000, bytes_accessed=4_000_000, transcendentals=4_000_000),
        name="mixer",
    )(
        inner_raw, pairs, gate_raw, step_raw.T, step_bias[None, :], rate_log[None, :],
        skip_gain[None, :], conv_inner, conv_pairs, norm_gain[None, :],
    )


def solution(mesh):
    placed = (
        P(("rollout", "context", "head"), None),
        P(("rollout", "context", "head"), None, None, None),
        P(("rollout", "context"), "head"),
        P(("rollout", "context"), "head"),
        P("head"),
        P("head"),
        P("head"),
        P(),
        P(),
        P("head"),
    )
    return jax.shard_map(
        on_device,
        mesh=mesh,
        in_specs=placed,
        out_specs=P(("rollout", "context", "head"), None),
        check_vma=False,
    )
```

```python
import functools

import jax
import jax.numpy as jnp
from jax import lax
from jax.experimental import pallas as pl
from jax.experimental.pallas import tpu as pltpu
from jax.sharding import PartitionSpec as P

BLOCK = 256
PAD = 16
CHUNK = 32
WIDE = 256
LOG2E = 1.4426950408889634
PIECE = 512
HOP = 128
BF = jnp.bfloat16
F32 = jnp.float32


def silu(v):
    half = 0.5 * v
    return half + half * jnp.tanh(half)


def conv_rows(src, dst, weight_of, taps, cols, wide):
    rows = src.shape[0] - PAD

    def step(i, carry):
        r0 = pl.multiple_of(i * CHUNK, CHUNK)
        for c0 in range(0, cols, wide):
            raw = src[pl.ds(r0, CHUNK + PAD), c0 : c0 + wide].astype(F32)
            w = weight_of(c0)
            total = w[taps]
            for k in range(taps):
                o = PAD - taps + k
                total = total + w[k] * raw[o : o + CHUNK]
            dst[pl.ds(r0, CHUNK), c0 : c0 + wide] = silu(total).astype(BF)
        return carry

    lax.fori_loop(0, rows // CHUNK, step, 0)


def kernel(
    n, nctx, groups, heads_local,
    inner, pairs, gate_hbm, step_raw, step_bias, rate_log, skip_gain, w_inner, w_pairs, norm_gain,
    out,
    gbuf, act, xraw, praw, xc, pc, mixed, ex, local, scores, cin, cout, outbuf,
    xs, xr, ps, pr, lsem, hs, hr, cs, cr, os, orr, olsem, gsem,
):
    me = lax.axis_index("head")
    ctx = lax.axis_index("context")
    rows = inner.shape[0]
    width = gate_hbm.shape[1]
    gate = gbuf
    gw = width // groups
    per = heads_local // groups
    hd = width // heads_local
    pw = praw.shape[1]
    st = pw // (2 * groups)
    pieces = gw // WIDE
    hops = WIDE // HOP
    count = width // PIECE

    gate_copy = pltpu.make_async_copy(gate_hbm, gbuf, gsem)
    gate_copy.start()

    barrier = pltpu.get_barrier_semaphore()
    for k in range(1, n):
        pl.semaphore_signal(barrier, inc=1, device_id={"head": lax.rem(me + k, n)})

    @pl.when(ctx > 0)
    def _():
        pl.semaphore_signal(barrier, inc=1, device_id={"context": ctx - 1})

    @pl.when(ctx < nctx - 1)
    def _():
        pl.semaphore_signal(barrier, inc=1, device_id={"context": ctx + 1})

    links = jnp.where(ctx > 0, 1, 0) + jnp.where(ctx < nctx - 1, 1, 0)
    pl.semaphore_wait(barrier, n - 1 + links)

    def p_copy(k, who, at):
        return pltpu.make_async_remote_copy(
            src_ref=pairs.at[:, pl.ds(pl.multiple_of(who * pw, 128), pw)],
            dst_ref=praw.at[pl.ds(pl.multiple_of(PAD + at * rows, 16), rows), :],
            send_sem=ps.at[k - 1], recv_sem=pr.at[k - 1], device_id={"head": who})

    def x_copy(q, k, who, at):
        return pltpu.make_async_remote_copy(
            src_ref=inner.at[:, pl.ds(pl.multiple_of(who * width + q * PIECE, 128), PIECE)],
            dst_ref=xraw.at[q, pl.ds(pl.multiple_of(PAD + at * rows, 16), rows), :],
            send_sem=xs.at[q, k - 1], recv_sem=xr.at[q, k - 1], device_id={"head": who})

    def o_copy(g, k, who, at):
        return pltpu.make_async_remote_copy(
            src_ref=outbuf.at[g, pl.ds(pl.multiple_of(who * rows, 16), rows), :],
            dst_ref=out.at[:, pl.ds(pl.multiple_of(at * width + g * gw, 128), gw)],
            send_sem=os.at[g, k - 1], recv_sem=orr.at[g, k - 1], device_id={"head": who})

    def halo(i, ref):
        last = ref.shape[0] - PAD
        return pltpu.make_async_remote_copy(
            src_ref=ref.at[last:, :], dst_ref=ref.at[0:PAD, :],
            send_sem=hs.at[i], recv_sem=hr.at[i],
            device_id={"context": lax.rem(ctx + 1, nctx)})

    def chain(g, p):
        return pltpu.make_async_remote_copy(
            src_ref=cout.at[g, p], dst_ref=cin.at[g, p],
            send_sem=cs.at[g, p], recv_sem=cr.at[g, p],
            device_id={"context": lax.rem(ctx + 1, nctx)})

    def to(k):
        return lax.rem(me + k, n)

    def source(k):
        return lax.rem(me + n - k, n)

    for k in range(1, n):
        p_copy(k, to(k), me).start()
    def send_x(q):
        if q < count:
            for k in range(1, n):
                x_copy(q, k, to(k), me).start()

    send_x(0)
    own_rows = pl.ds(pl.multiple_of(PAD + me * rows, 16), rows)
    own = [pltpu.make_async_copy(
        pairs.at[:, pl.ds(pl.multiple_of(me * pw, 128), pw)], praw.at[own_rows, :], lsem.at[0])]
    for q in range(count):
        own.append(pltpu.make_async_copy(
            inner.at[:, pl.ds(pl.multiple_of(me * width + q * PIECE, 128), PIECE)],
            xraw.at[q, own_rows, :], lsem.at[1 + q]))
    for c in own:
        c.start()

    @pl.when(ctx == 0)
    def _():
        praw[0:PAD, :] = jnp.zeros((PAD, pw), BF)
        for q in range(count):
            xraw[q, 0:PAD, :] = jnp.zeros((PAD, PIECE), BF)

    v = step_raw[...].astype(F32) + step_bias[...].T
    step = jnp.maximum(v, 0.0) + jnp.log1p(jnp.exp(-jnp.abs(v)))
    tri_r = lax.broadcasted_iota(jnp.int32, (BLOCK, BLOCK), 0)
    tri_c = lax.broadcasted_iota(jnp.int32, (BLOCK, BLOCK), 1)
    lower = tri_r >= tri_c
    lc_t = jnp.dot(-jnp.exp(rate_log[...].T) * step, (tri_r <= tri_c).astype(F32),
                   precision=lax.Precision.HIGHEST, preferred_element_type=F32)
    shifted_t = lc_t - jnp.log(step)
    lc = lc_t.T
    shifted = shifted_t.T
    tail = jnp.exp(lc[BLOCK - 1 : BLOCK, :] - shifted)
    grow = jnp.exp(lc)

    lc2 = lc * LOG2E
    shifted2_t = shifted_t * LOG2E

    def spread(cols, a):
        left = lax.broadcasted_iota(jnp.int32, (cols.shape[0], 2 * hd), 1) < hd
        return jnp.where(left, cols[:, a : a + 1], cols[:, a + 1 : a + 2])

    def arrived(i, ref, waits, own_copy):
        for w in waits:
            w.wait_recv()
        send_x(i + 1)
        own_copy.wait()

        @pl.when(ctx < nctx - 1)
        def _():
            halo(i, ref).start()

        @pl.when(ctx > 0)
        def _():
            halo(i, ref).wait_recv()

    for g in range(groups):
        for a in range(0, per, 2):
            ex[g, :, a * hd : (a + 2) * hd] = spread(grow, g * per + a)

    gate_copy.wait()

    def open_gate(i, carry):
        at = pl.ds(pl.multiple_of(i * CHUNK, CHUNK), CHUNK)
        for c0 in range(0, width, WIDE):
            act[at, c0 : c0 + WIDE] = silu(gate[at, c0 : c0 + WIDE].astype(F32))
        return carry

    lax.fori_loop(0, BLOCK // CHUNK, open_gate, 0)
    arrived(0, praw, [p_copy(k, to(k), source(k)) for k in range(1, n)], own[0])
    taps = w_inner.shape[0] - 1

    def pair_weight(c0):
        g, b = divmod(c0 // st, 2)
        return [w_pairs[k, me * groups + g, b : b + 1, :] for k in range(taps + 1)]

    def inner_weight(q):
        def rows_at(c0):
            at = pl.ds(pl.multiple_of(me * width + q * PIECE + c0, WIDE), WIDE)
            return [w_inner[k : k + 1, at] for k in range(taps + 1)]

        return rows_at

    conv_rows(praw, pc, pair_weight, taps, pw, st)
    bts = []
    for g in range(groups):
        bt = pc[:, 2 * g * st : (2 * g + 1) * st].astype(F32).T.astype(BF)
        bts.append(bt)
        raw_scores = jnp.dot(
            pc[:, (2 * g + 1) * st : (2 * g + 2) * st], bt, preferred_element_type=F32)
        scores[g] = jnp.where(lower, raw_scores, 0.0)

    def prepare(q):
        arrived(1 + q, xraw.at[q],
                [x_copy(q, k, to(k), source(k)) for k in range(1, n)], own[1 + q])
        conv_rows(xraw.at[q], xc.at[q], inner_weight(q), taps, PIECE, WIDE)
        for c0 in range(0, PIECE, WIDE):
            g, first = divmod(q * PIECE + c0, gw)
            p = first // WIDE
            parts = []
            for o in range(c0, c0 + WIDE, 2 * hd):
                x = xc[q, :, o : o + 2 * hd].astype(F32)
                parts.append((x * spread(tail, (q * PIECE + o) // hd)).astype(BF))
            weighted = jnp.concatenate(parts, axis=1)
            state = jnp.dot(bts[g], weighted, preferred_element_type=F32)
            local[g, p] = state

            @pl.when(ctx == 0)
            def _():
                for j in range(hops):
                    cout[g, p * hops + j] = state[:, j * HOP : (j + 1) * HOP].astype(BF)
                    if nctx > 1:
                        chain(g, p * hops + j).start()

    half = BLOCK // 2

    def intra(g, a):
        q, o = divmod(g * gw + a * hd, PIECE)
        x = xc[q, :, o : o + 2 * hd]
        top, low = [], []
        for b in (a, a + 1):
            h = g * per + b
            col = lc2[:, h : h + 1]
            row = shifted2_t[h : h + 1, :]
            w0 = scores[g, :half, :half] * jnp.exp2(jnp.minimum(col[:half] - row[:, :half], 40.0))
            top.append(jnp.dot(w0.astype(BF), x[:half], preferred_element_type=F32))
            w1 = scores[g, half:, :half] * jnp.exp2(col[half:] - row[:, :half])
            w2 = scores[g, half:, half:] * jnp.exp2(jnp.minimum(col[half:] - row[:, half:], 40.0))
            w = jnp.concatenate([w1.astype(BF), w2.astype(BF)], axis=1)
            low.append(jnp.dot(w, x, preferred_element_type=F32))
        left = lax.broadcasted_iota(jnp.int32, (half, 2 * hd), 1) < hd
        gain = spread(skip_gain[...], g * per + a)
        xf = x.astype(F32) * gain
        mixed[g, :half, a * hd : (a + 2) * hd] = jnp.where(left, top[0], top[1]) + xf[:half]
        mixed[g, half:, a * hd : (a + 2) * hd] = jnp.where(left, low[0], low[1]) + xf[half:]

    def forward(g, p):
        @pl.when(jnp.logical_and(ctx > 0, ctx < nctx - 1))
        def _():
            for j in range(hops):
                c = p * hops + j
                chain(g, c).wait_recv()
                decay = ex[g, BLOCK - 1 : BLOCK, c * HOP : (c + 1) * HOP]
                own_state = local[g, p, :, j * HOP : (j + 1) * HOP]
                cout[g, c] = (decay * cin[g, c].astype(F32) + own_state).astype(BF)
                chain(g, c).start()

    def absorb(g):
        @pl.when(ctx > 0)
        def _():
            for p in range(pieces):
                cols = slice(p * WIDE, (p + 1) * WIDE)

                @pl.when(ctx == nctx - 1)
                def _():
                    for j in range(hops):
                        chain(g, p * hops + j).wait_recv()

                cmat = pc[:, (2 * g + 1) * st : (2 * g + 2) * st]
                held = jnp.concatenate([cin[g, p * hops + j] for j in range(hops)], axis=1)
                carried = jnp.dot(cmat, held, preferred_element_type=F32)
                mixed[g, :, cols] = mixed[g, :, cols] + carried * ex[g, :, cols]

    own_out = []

    def finish(g):
        for k in list(range(1, n)) + [0]:
            who = to(k)
            rs = pl.ds(pl.multiple_of(who * rows, rows), rows)
            ssq = jnp.zeros((rows, 1), F32)
            for p in range(pieces):
                cols = slice(p * WIDE, (p + 1) * WIDE)
                z = act[rs, g * gw + p * WIDE : g * gw + (p + 1) * WIDE]
                gated = mixed[g, rs, cols] * z
                mixed[g, rs, cols] = gated
                ssq = ssq + jnp.sum(gated * gated, axis=1, keepdims=True)
            inv = lax.rsqrt(ssq / gw + 1e-05)
            for p in range(pieces):
                cols = slice(p * WIDE, (p + 1) * WIDE)
                gain = norm_gain[:, g * gw + p * WIDE : g * gw + (p + 1) * WIDE]
                outbuf[g, rs, cols] = (mixed[g, rs, cols] * inv * gain).astype(BF)
            if k:
                o_copy(g, k, who, me).start()
            else:
                c = pltpu.make_async_copy(
                    outbuf.at[g, rs, :],
                    out.at[:, pl.ds(pl.multiple_of(me * width + g * gw, 128), gw)], olsem.at[g])
                c.start()
                own_out.append(c)

    def pieces_of(q):
        return [divmod(c0, gw) for c0 in range(q * PIECE, (q + 1) * PIECE, WIDE)]

    def intra_piece(q):
        for g, first in pieces_of(q):
            for a in range(first // hd, (first + WIDE) // hd, 2):
                intra(g, a)

    def forward_piece(q):
        for g, first in pieces_of(q):
            forward(g, first // WIDE)

    prepare(0)
    intra_piece(0)
    for q in range(1, count):
        prepare(q)
        forward_piece(q - 1)
    per_group = gw // PIECE
    for q in range(1, count):
        intra_piece(q)
        if q == 1:
            forward_piece(count - 1)
        if q % per_group == per_group - 1:
            absorb(q // per_group)
            finish(q // per_group)

    for k in range(1, n):
        p_copy(k, to(k), me).wait_send()
        for q in range(count):
            x_copy(q, k, to(k), me).wait_send()
        for g in range(groups):
            o_copy(g, k, to(k), me).wait_send()
            o_copy(g, k, to(k), source(k)).wait_recv()
    for c in own_out:
        c.wait()

    @pl.when(ctx < nctx - 1)
    def _():
        halo(0, praw).wait_send()
        for q in range(count):
            halo(1 + q, xraw.at[q]).wait_send()
        for g in range(groups):
            for c in range(pieces * hops):
                chain(g, c).wait_send()


def on_device(
    inner_raw, pairs_raw, gate_raw, step_raw, step_bias, rate_log,
    skip_gain, conv_inner, conv_pairs, norm_gain,
):
    n = lax.axis_size("head")
    nctx = lax.axis_size("context")
    rows, full = inner_raw.shape
    width = gate_raw.shape[1]
    heads = step_raw.shape[1]
    groups = pairs_raw.shape[1] // n
    st = pairs_raw.shape[3]
    pw = groups * 2 * st
    gw = width // groups
    pieces = gw // WIDE
    count = width // PIECE
    pairs = pairs_raw.reshape(rows, -1)
    vm = pl.BlockSpec(memory_space=pltpu.VMEM)
    hbm = pl.BlockSpec(memory_space=pl.ANY)
    far = pl.BlockSpec(memory_space=pltpu.MemorySpace.HBM)
    dma = pltpu.SemaphoreType.DMA
    return pl.pallas_call(
        functools.partial(kernel, n, nctx, groups, heads),
        out_shape=jax.ShapeDtypeStruct((rows, full), BF),
        in_specs=[far, hbm, far] + [vm] * 7,
        out_specs=hbm,
        scratch_shapes=[
            pltpu.VMEM((BLOCK, width), BF),
            pltpu.VMEM((BLOCK, width), F32),
            pltpu.VMEM((count, PAD + BLOCK, PIECE), BF),
            pltpu.VMEM((PAD + BLOCK, pw), BF),
            pltpu.VMEM((count, BLOCK, PIECE), BF),
            pltpu.VMEM((BLOCK, pw), BF),
            pltpu.VMEM((groups, BLOCK, gw), F32),
            pltpu.VMEM((groups, BLOCK, gw), F32),
            pltpu.VMEM((groups, pieces, st, WIDE), F32),
            pltpu.VMEM((groups, BLOCK, BLOCK), F32),
            pltpu.VMEM((groups, gw // HOP, st, HOP), BF),
            pltpu.VMEM((groups, gw // HOP, st, HOP), BF),
            pltpu.VMEM((groups, BLOCK, gw), BF),
            dma((count, n - 1)), dma((count, n - 1)),
            dma((n - 1,)), dma((n - 1,)),
            dma((1 + count,)),
            dma((1 + count,)), dma((1 + count,)),
            dma((groups, gw // HOP)), dma((groups, gw // HOP)),
            dma((groups, n - 1)), dma((groups, n - 1)),
            dma((groups,)),
            dma,
        ],
        compiler_params=pltpu.CompilerParams(
            collective_id=0, has_side_effects=True, vmem_limit_bytes=58 * 1024 * 1024),
        cost_estimate=pl.CostEstimate(
            flops=700_000_000, bytes_accessed=4_000_000, transcendentals=4_000_000),
        name="mixer",
    )(
        inner_raw, pairs, gate_raw, step_raw.T, step_bias[None, :], rate_log[None, :],
        skip_gain[None, :], conv_inner, conv_pairs, norm_gain[None, :],
    )


def solution(mesh):
    placed = (
        P(("rollout", "context", "head"), None),
        P(("rollout", "context", "head"), None, None, None),
        P(("rollout", "context"), "head"),
        P(("rollout", "context"), "head"),
        P("head"),
        P("head"),
        P("head"),
        P(),
        P(),
        P("head"),
    )
    return jax.shard_map(
        on_device,
        mesh=mesh,
        in_specs=placed,
        out_specs=P(("rollout", "context", "head"), None),
        check_vma=False,
    )
```

```python
import functools

import jax
import jax.numpy as jnp
from jax import lax
from jax.experimental import pallas as pl
from jax.experimental.pallas import tpu as pltpu
from jax.sharding import PartitionSpec as P

BLOCK = 256
PAD = 16
CHUNK = 32
WIDE = 256
LOG2E = 1.4426950408889634
PIECE = 512
HOP = 128
BF = jnp.bfloat16
F32 = jnp.float32


def silu(v):
    half = 0.5 * v
    return half + half * jnp.tanh(half)


def conv_rows(src, dst, weight_of, taps, cols, wide):
    rows = src.shape[0] - PAD

    def step(i, carry):
        r0 = pl.multiple_of(i * CHUNK, CHUNK)
        for c0 in range(0, cols, wide):
            raw = src[pl.ds(r0, CHUNK + PAD), c0 : c0 + wide].astype(F32)
            w = weight_of(c0)
            total = w[taps]
            for k in range(taps):
                o = PAD - taps + k
                total = total + w[k] * raw[o : o + CHUNK]
            dst[pl.ds(r0, CHUNK), c0 : c0 + wide] = silu(total).astype(BF)
        return carry

    lax.fori_loop(0, rows // CHUNK, step, 0)


def kernel(
    n, nctx, groups, heads_local,
    inner, pairs, gate_hbm, step_raw, step_bias, rate_log, skip_gain, w_inner, w_pairs, norm_gain,
    out,
    gbuf, act, xraw, praw, xc, pc, mixed, ex, local, scores, cin, cout, outbuf,
    xs, xr, ps, pr, lsem, hs, hr, cs, cr, os, orr, olsem, gsem,
):
    me = lax.axis_index("head")
    ctx = lax.axis_index("context")
    rows = inner.shape[0]
    width = gate_hbm.shape[1]
    gate = gbuf
    gw = width // groups
    per = heads_local // groups
    hd = width // heads_local
    pw = praw.shape[1]
    st = pw // (2 * groups)
    pieces = gw // WIDE
    hops = WIDE // HOP
    count = width // PIECE

    gate_copy = pltpu.make_async_copy(gate_hbm, gbuf, gsem)
    gate_copy.start()

    barrier = pltpu.get_barrier_semaphore()
    for k in range(1, n):
        pl.semaphore_signal(barrier, inc=1, device_id={"head": lax.rem(me + k, n)})

    @pl.when(ctx > 0)
    def _():
        pl.semaphore_signal(barrier, inc=1, device_id={"context": ctx - 1})

    @pl.when(ctx < nctx - 1)
    def _():
        pl.semaphore_signal(barrier, inc=1, device_id={"context": ctx + 1})

    links = jnp.where(ctx > 0, 1, 0) + jnp.where(ctx < nctx - 1, 1, 0)
    pl.semaphore_wait(barrier, n - 1 + links)

    def p_copy(k, who, at):
        return pltpu.make_async_remote_copy(
            src_ref=pairs.at[:, pl.ds(pl.multiple_of(who * pw, 128), pw)],
            dst_ref=praw.at[pl.ds(pl.multiple_of(PAD + at * rows, 16), rows), :],
            send_sem=ps.at[k - 1], recv_sem=pr.at[k - 1], device_id={"head": who})

    def x_copy(q, k, who, at):
        return pltpu.make_async_remote_copy(
            src_ref=inner.at[:, pl.ds(pl.multiple_of(who * width + q * PIECE, 128), PIECE)],
            dst_ref=xraw.at[q, pl.ds(pl.multiple_of(PAD + at * rows, 16), rows), :],
            send_sem=xs.at[q, k - 1], recv_sem=xr.at[q, k - 1], device_id={"head": who})

    def o_copy(g, k, who, at):
        return pltpu.make_async_remote_copy(
            src_ref=outbuf.at[g, pl.ds(pl.multiple_of(who * rows, 16), rows), :],
            dst_ref=out.at[:, pl.ds(pl.multiple_of(at * width + g * gw, 128), gw)],
            send_sem=os.at[g, k - 1], recv_sem=orr.at[g, k - 1], device_id={"head": who})

    def halo(i, ref):
        last = ref.shape[0] - PAD
        return pltpu.make_async_remote_copy(
            src_ref=ref.at[last:, :], dst_ref=ref.at[0:PAD, :],
            send_sem=hs.at[i], recv_sem=hr.at[i],
            device_id={"context": lax.rem(ctx + 1, nctx)})

    def chain(g, p):
        return pltpu.make_async_remote_copy(
            src_ref=cout.at[g, p], dst_ref=cin.at[g, p],
            send_sem=cs.at[g, p], recv_sem=cr.at[g, p],
            device_id={"context": lax.rem(ctx + 1, nctx)})

    def to(k):
        return lax.rem(me + k, n)

    def source(k):
        return lax.rem(me + n - k, n)

    for k in range(1, n):
        p_copy(k, to(k), me).start()
    def send_x(q):
        if q < count:
            for k in range(1, n):
                x_copy(q, k, to(k), me).start()

    send_x(0)
    own_rows = pl.ds(pl.multiple_of(PAD + me * rows, 16), rows)
    own = [pltpu.make_async_copy(
        pairs.at[:, pl.ds(pl.multiple_of(me * pw, 128), pw)], praw.at[own_rows, :], lsem.at[0])]
    for q in range(count):
        own.append(pltpu.make_async_copy(
            inner.at[:, pl.ds(pl.multiple_of(me * width + q * PIECE, 128), PIECE)],
            xraw.at[q, own_rows, :], lsem.at[1 + q]))
    for c in own:
        c.start()

    @pl.when(ctx == 0)
    def _():
        praw[0:PAD, :] = jnp.zeros((PAD, pw), BF)
        for q in range(count):
            xraw[q, 0:PAD, :] = jnp.zeros((PAD, PIECE), BF)

    v = step_raw[...].astype(F32) + step_bias[...].T
    step = jnp.maximum(v, 0.0) + jnp.log1p(jnp.exp(-jnp.abs(v)))
    tri_r = lax.broadcasted_iota(jnp.int32, (BLOCK, BLOCK), 0)
    tri_c = lax.broadcasted_iota(jnp.int32, (BLOCK, BLOCK), 1)
    lower = tri_r >= tri_c
    lc_t = jnp.dot(-jnp.exp(rate_log[...].T) * step, (tri_r <= tri_c).astype(F32),
                   precision=lax.Precision.HIGHEST, preferred_element_type=F32)
    shifted_t = lc_t - jnp.log(step)
    lc = lc_t.T
    shifted = shifted_t.T
    tail = jnp.exp(lc[BLOCK - 1 : BLOCK, :] - shifted)
    grow = jnp.exp(lc)

    lc2 = lc * LOG2E
    shifted2_t = shifted_t * LOG2E

    def spread(cols, a):
        left = lax.broadcasted_iota(jnp.int32, (cols.shape[0], 2 * hd), 1) < hd
        return jnp.where(left, cols[:, a : a + 1], cols[:, a + 1 : a + 2])

    def arrived(i, ref, waits, own_copy):
        for w in waits:
            w.wait_recv()
        send_x(i + 1)
        own_copy.wait()

        @pl.when(ctx < nctx - 1)
        def _():
            halo(i, ref).start()

        @pl.when(ctx > 0)
        def _():
            halo(i, ref).wait_recv()

    for g in range(groups):
        for a in range(0, per, 2):
            ex[g, :, a * hd : (a + 2) * hd] = spread(grow, g * per + a)

    gate_copy.wait()

    def open_gate(i, carry):
        at = pl.ds(pl.multiple_of(i * CHUNK, CHUNK), CHUNK)
        for c0 in range(0, width, WIDE):
            act[at, c0 : c0 + WIDE] = silu(gate[at, c0 : c0 + WIDE].astype(F32))
        return carry

    lax.fori_loop(0, BLOCK // CHUNK, open_gate, 0)
    arrived(0, praw, [p_copy(k, to(k), source(k)) for k in range(1, n)], own[0])
    taps = w_inner.shape[0] - 1

    def pair_weight(c0):
        g, b = divmod(c0 // st, 2)
        return [w_pairs[k, me * groups + g, b : b + 1, :] for k in range(taps + 1)]

    def inner_weight(q):
        def rows_at(c0):
            at = pl.ds(pl.multiple_of(me * width + q * PIECE + c0, WIDE), WIDE)
            return [w_inner[k : k + 1, at] for k in range(taps + 1)]

        return rows_at

    conv_rows(praw, pc, pair_weight, taps, pw, st)
    bts = []
    for g in range(groups):
        bt = pc[:, 2 * g * st : (2 * g + 1) * st].astype(F32).T.astype(BF)
        bts.append(bt)
        raw_scores = jnp.dot(
            pc[:, (2 * g + 1) * st : (2 * g + 2) * st], bt, preferred_element_type=F32)
        scores[g] = jnp.where(lower, raw_scores, 0.0)

    def prepare(q):
        arrived(1 + q, xraw.at[q],
                [x_copy(q, k, to(k), source(k)) for k in range(1, n)], own[1 + q])
        conv_rows(xraw.at[q], xc.at[q], inner_weight(q), taps, PIECE, WIDE)
        for c0 in range(0, PIECE, WIDE):
            g, first = divmod(q * PIECE + c0, gw)
            p = first // WIDE
            parts = []
            for o in range(c0, c0 + WIDE, 2 * hd):
                x = xc[q, :, o : o + 2 * hd].astype(F32)
                parts.append((x * spread(tail, (q * PIECE + o) // hd)).astype(BF))
            weighted = jnp.concatenate(parts, axis=1)
            state = jnp.dot(bts[g], weighted, preferred_element_type=F32)
            local[g, p] = state

            @pl.when(ctx == 0)
            def _():
                for j in range(hops):
                    cout[g, p * hops + j] = state[:, j * HOP : (j + 1) * HOP].astype(BF)
                    if nctx > 1:
                        chain(g, p * hops + j).start()

    half = BLOCK // 2

    def intra(g, a):
        q, o = divmod(g * gw + a * hd, PIECE)
        x = xc[q, :, o : o + 2 * hd]
        top, low = [], []
        for b in (a, a + 1):
            h = g * per + b
            col = lc2[:, h : h + 1]
            row = shifted2_t[h : h + 1, :]
            w0 = scores[g, :half, :half] * jnp.exp2(jnp.minimum(col[:half] - row[:, :half], 40.0))
            top.append(jnp.dot(w0.astype(BF), x[:half], preferred_element_type=F32))
            w1 = scores[g, half:, :half] * jnp.exp2(col[half:] - row[:, :half])
            w2 = scores[g, half:, half:] * jnp.exp2(jnp.minimum(col[half:] - row[:, half:], 40.0))
            w = jnp.concatenate([w1.astype(BF), w2.astype(BF)], axis=1)
            low.append(jnp.dot(w, x, preferred_element_type=F32))
        left = lax.broadcasted_iota(jnp.int32, (half, 2 * hd), 1) < hd
        gain = spread(skip_gain[...], g * per + a)
        xf = x.astype(F32) * gain
        mixed[g, :half, a * hd : (a + 2) * hd] = jnp.where(left, top[0], top[1]) + xf[:half]
        mixed[g, half:, a * hd : (a + 2) * hd] = jnp.where(left, low[0], low[1]) + xf[half:]

    def forward(g, p, chosen):
        @pl.when(jnp.logical_and(chosen, ctx < nctx - 1))
        def _():
            for j in range(hops):
                c = p * hops + j
                chain(g, c).wait_recv()
                decay = ex[g, BLOCK - 1 : BLOCK, c * HOP : (c + 1) * HOP]
                own_state = local[g, p, :, j * HOP : (j + 1) * HOP]
                cout[g, c] = (decay * cin[g, c].astype(F32) + own_state).astype(BF)
                chain(g, c).start()

    def absorb(g):
        @pl.when(ctx > 0)
        def _():
            for p in range(pieces):
                cols = slice(p * WIDE, (p + 1) * WIDE)

                @pl.when(ctx == nctx - 1)
                def _():
                    for j in range(hops):
                        chain(g, p * hops + j).wait_recv()

                cmat = pc[:, (2 * g + 1) * st : (2 * g + 2) * st]
                held = jnp.concatenate([cin[g, p * hops + j] for j in range(hops)], axis=1)
                carried = jnp.dot(cmat, held, preferred_element_type=F32)
                mixed[g, :, cols] = mixed[g, :, cols] + carried * ex[g, :, cols]

    own_out = []

    def finish(g):
        for k in list(range(1, n)) + [0]:
            who = to(k)
            rs = pl.ds(pl.multiple_of(who * rows, rows), rows)
            ssq = jnp.zeros((rows, 1), F32)
            for p in range(pieces):
                cols = slice(p * WIDE, (p + 1) * WIDE)
                z = act[rs, g * gw + p * WIDE : g * gw + (p + 1) * WIDE]
                gated = mixed[g, rs, cols] * z
                mixed[g, rs, cols] = gated
                ssq = ssq + jnp.sum(gated * gated, axis=1, keepdims=True)
            inv = lax.rsqrt(ssq / gw + 1e-05)
            for p in range(pieces):
                cols = slice(p * WIDE, (p + 1) * WIDE)
                gain = norm_gain[:, g * gw + p * WIDE : g * gw + (p + 1) * WIDE]
                outbuf[g, rs, cols] = (mixed[g, rs, cols] * inv * gain).astype(BF)
            if k:
                o_copy(g, k, who, me).start()
            else:
                c = pltpu.make_async_copy(
                    outbuf.at[g, rs, :],
                    out.at[:, pl.ds(pl.multiple_of(me * width + g * gw, 128), gw)], olsem.at[g])
                c.start()
                own_out.append(c)

    def pieces_of(q):
        return [divmod(c0, gw) for c0 in range(q * PIECE, (q + 1) * PIECE, WIDE)]

    def intra_piece(q):
        for g, first in pieces_of(q):
            for a in range(first // hd, (first + WIDE) // hd, 2):
                intra(g, a)

    def forward_piece(q, chosen):
        for g, first in pieces_of(q):
            forward(g, first // WIDE, chosen)

    near, far = ctx == 1, ctx > 1

    prepare(0)
    intra_piece(0)
    for q in range(1, count):
        prepare(q)
        forward_piece(q - 1, near)
        if q > 1:
            forward_piece(q - 2, far)
    per_group = gw // PIECE
    for q in range(1, count):
        intra_piece(q)
        if q == 1:
            forward_piece(count - 1, near)
            forward_piece(count - 2, far)
        if q % per_group == per_group - 1:
            absorb(q // per_group)
            finish(q // per_group)
        if q == 1:
            forward_piece(count - 1, far)

    for k in range(1, n):
        p_copy(k, to(k), me).wait_send()
        for q in range(count):
            x_copy(q, k, to(k), me).wait_send()
        for g in range(groups):
            o_copy(g, k, to(k), me).wait_send()
            o_copy(g, k, to(k), source(k)).wait_recv()
    for c in own_out:
        c.wait()

    @pl.when(ctx < nctx - 1)
    def _():
        halo(0, praw).wait_send()
        for q in range(count):
            halo(1 + q, xraw.at[q]).wait_send()
        for g in range(groups):
            for c in range(pieces * hops):
                chain(g, c).wait_send()


def on_device(
    inner_raw, pairs_raw, gate_raw, step_raw, step_bias, rate_log,
    skip_gain, conv_inner, conv_pairs, norm_gain,
):
    n = lax.axis_size("head")
    nctx = lax.axis_size("context")
    rows, full = inner_raw.shape
    width = gate_raw.shape[1]
    heads = step_raw.shape[1]
    groups = pairs_raw.shape[1] // n
    st = pairs_raw.shape[3]
    pw = groups * 2 * st
    gw = width // groups
    pieces = gw // WIDE
    count = width // PIECE
    pairs = pairs_raw.reshape(rows, -1)
    vm = pl.BlockSpec(memory_space=pltpu.VMEM)
    hbm = pl.BlockSpec(memory_space=pl.ANY)
    far = pl.BlockSpec(memory_space=pltpu.MemorySpace.HBM)
    dma = pltpu.SemaphoreType.DMA
    return pl.pallas_call(
        functools.partial(kernel, n, nctx, groups, heads),
        out_shape=jax.ShapeDtypeStruct((rows, full), BF),
        in_specs=[far, hbm, far] + [vm] * 7,
        out_specs=hbm,
        scratch_shapes=[
            pltpu.VMEM((BLOCK, width), BF),
            pltpu.VMEM((BLOCK, width), F32),
            pltpu.VMEM((count, PAD + BLOCK, PIECE), BF),
            pltpu.VMEM((PAD + BLOCK, pw), BF),
            pltpu.VMEM((count, BLOCK, PIECE), BF),
            pltpu.VMEM((BLOCK, pw), BF),
            pltpu.VMEM((groups, BLOCK, gw), F32),
            pltpu.VMEM((groups, BLOCK, gw), F32),
            pltpu.VMEM((groups, pieces, st, WIDE), F32),
            pltpu.VMEM((groups, BLOCK, BLOCK), F32),
            pltpu.VMEM((groups, gw // HOP, st, HOP), BF),
            pltpu.VMEM((groups, gw // HOP, st, HOP), BF),
            pltpu.VMEM((groups, BLOCK, gw), BF),
            dma((count, n - 1)), dma((count, n - 1)),
            dma((n - 1,)), dma((n - 1,)),
            dma((1 + count,)),
            dma((1 + count,)), dma((1 + count,)),
            dma((groups, gw // HOP)), dma((groups, gw // HOP)),
            dma((groups, n - 1)), dma((groups, n - 1)),
            dma((groups,)),
            dma,
        ],
        compiler_params=pltpu.CompilerParams(
            collective_id=0, has_side_effects=True, vmem_limit_bytes=58 * 1024 * 1024),
        cost_estimate=pl.CostEstimate(
            flops=700_000_000, bytes_accessed=4_000_000, transcendentals=4_000_000),
        name="mixer",
    )(
        inner_raw, pairs, gate_raw, step_raw.T, step_bias[None, :], rate_log[None, :],
        skip_gain[None, :], conv_inner, conv_pairs, norm_gain[None, :],
    )


def solution(mesh):
    placed = (
        P(("rollout", "context", "head"), None),
        P(("rollout", "context", "head"), None, None, None),
        P(("rollout", "context"), "head"),
        P(("rollout", "context"), "head"),
        P("head"),
        P("head"),
        P("head"),
        P(),
        P(),
        P("head"),
    )
    return jax.shard_map(
        on_device,
        mesh=mesh,
        in_specs=placed,
        out_specs=P(("rollout", "context", "head"), None),
        check_vma=False,
    )
```

```python
import functools

import jax
import jax.numpy as jnp
from jax import lax
from jax.experimental import pallas as pl
from jax.experimental.pallas import tpu as pltpu
from jax.sharding import PartitionSpec as P

BLOCK = 256
PAD = 16
CHUNK = 32
WIDE = 256
BF = jnp.bfloat16
F32 = jnp.float32


def silu(v):
    half = 0.5 * v
    return half + half * jnp.tanh(half)


def conv_rows(src, dst, weight, first_col, cols, dst_of):
    rows = src.shape[0] - PAD
    taps = weight.shape[0] - 1

    def step(i, carry):
        r0 = pl.multiple_of(i * CHUNK, CHUNK)
        for c0 in range(0, cols, WIDE):
            raw = src[pl.ds(r0, CHUNK + PAD), c0 : c0 + WIDE].astype(F32)
            w = weight[:, pl.ds(pl.multiple_of(first_col + c0, WIDE), WIDE)]
            total = w[taps : taps + 1]
            for k in range(taps):
                o = PAD - taps + k
                total = total + w[k : k + 1] * raw[o : o + CHUNK]
            dst_of(dst, r0, c0, silu(total).astype(BF))
        return carry

    lax.fori_loop(0, rows // CHUNK, step, 0)


def store_plain(dst, r0, c0, value):
    dst[pl.ds(r0, CHUNK), c0 : c0 + WIDE] = value


def kernel(
    n, nctx, groups, heads_local,
    inner, pairs, gate_hbm, step_raw, step_bias, rate_log, skip_gain, w_inner, w_pairs, norm_gain,
    out,
    gate, xraw, praw, xc, pc, mixed, ex, local, scores, cin, cout, outbuf,
    xs, xr, ps, pr, lsem, hs, hr, cs, cr, os, orr, olsem, gsem,
):
    me = lax.axis_index("head")
    ctx = lax.axis_index("context")
    rows = inner.shape[0]
    width = gate.shape[1]
    gw = width // groups
    per = heads_local // groups
    hd = width // heads_local
    pw = praw.shape[1]
    st = pw // (2 * groups)
    pieces = gw // WIDE

    gate_copy = pltpu.make_async_copy(gate_hbm, gate, gsem)
    gate_copy.start()

    barrier = pltpu.get_barrier_semaphore()
    for k in range(1, n):
        pl.semaphore_signal(barrier, inc=1, device_id={"head": lax.rem(me + k, n)})

    @pl.when(ctx > 0)
    def _():
        pl.semaphore_signal(barrier, inc=1, device_id={"context": ctx - 1})

    @pl.when(ctx < nctx - 1)
    def _():
        pl.semaphore_signal(barrier, inc=1, device_id={"context": ctx + 1})

    links = jnp.where(ctx > 0, 1, 0) + jnp.where(ctx < nctx - 1, 1, 0)
    pl.semaphore_wait(barrier, n - 1 + links)

    def p_copy(k, who, at):
        return pltpu.make_async_remote_copy(
            src_ref=pairs.at[:, pl.ds(pl.multiple_of(who * pw, 128), pw)],
            dst_ref=praw.at[pl.ds(pl.multiple_of(PAD + at * rows, 16), rows), :],
            send_sem=ps.at[k - 1], recv_sem=pr.at[k - 1], device_id={"head": who})

    def x_copy(g, k, who, at):
        return pltpu.make_async_remote_copy(
            src_ref=inner.at[:, pl.ds(pl.multiple_of(who * width + g * gw, 128), gw)],
            dst_ref=xraw.at[g, pl.ds(pl.multiple_of(PAD + at * rows, 16), rows), :],
            send_sem=xs.at[g, k - 1], recv_sem=xr.at[g, k - 1], device_id={"head": who})

    def o_copy(g, k, who, at):
        return pltpu.make_async_remote_copy(
            src_ref=outbuf.at[g, pl.ds(pl.multiple_of(who * rows, 16), rows), :],
            dst_ref=out.at[:, pl.ds(pl.multiple_of(at * width + g * gw, 128), gw)],
            send_sem=os.at[g, k - 1], recv_sem=orr.at[g, k - 1], device_id={"head": who})

    def halo(i, ref):
        last = ref.shape[0] - PAD
        return pltpu.make_async_remote_copy(
            src_ref=ref.at[last:, :], dst_ref=ref.at[0:PAD, :],
            send_sem=hs.at[i], recv_sem=hr.at[i],
            device_id={"context": lax.rem(ctx + 1, nctx)})

    def chain(g, p):
        return pltpu.make_async_remote_copy(
            src_ref=cout.at[g, p], dst_ref=cin.at[g, p],
            send_sem=cs.at[g, p], recv_sem=cr.at[g, p],
            device_id={"context": lax.rem(ctx + 1, nctx)})

    def to(k):
        return lax.rem(me + k, n)

    def source(k):
        return lax.rem(me + n - k, n)

    for k in range(1, n):
        p_copy(k, to(k), me).start()
    for g in range(groups):
        for k in range(1, n):
            x_copy(g, k, to(k), me).start()
    own_rows = pl.ds(pl.multiple_of(PAD + me * rows, 16), rows)
    own = [pltpu.make_async_copy(
        pairs.at[:, pl.ds(pl.multiple_of(me * pw, 128), pw)], praw.at[own_rows, :], lsem.at[0])]
    for g in range(groups):
        own.append(pltpu.make_async_copy(
            inner.at[:, pl.ds(pl.multiple_of(me * width + g * gw, 128), gw)],
            xraw.at[g, own_rows, :], lsem.at[1 + g]))
    for c in own:
        c.start()

    @pl.when(ctx == 0)
    def _():
        praw[0:PAD, :] = jnp.zeros((PAD, pw), BF)
        for g in range(groups):
            xraw[g, 0:PAD, :] = jnp.zeros((PAD, gw), BF)

    v = step_raw[...].astype(F32) + step_bias[...].T
    step = jnp.maximum(v, 0.0) + jnp.log1p(jnp.exp(-jnp.abs(v)))
    tri_r = lax.broadcasted_iota(jnp.int32, (BLOCK, BLOCK), 0)
    tri_c = lax.broadcasted_iota(jnp.int32, (BLOCK, BLOCK), 1)
    lower = tri_r >= tri_c
    lc_t = jnp.dot(-jnp.exp(rate_log[...].T) * step, (tri_r <= tri_c).astype(F32),
                   precision=lax.Precision.HIGHEST, preferred_element_type=F32)
    shifted_t = lc_t - jnp.log(step)
    lc = lc_t.T
    shifted = shifted_t.T
    tail = jnp.exp(lc[BLOCK - 1 : BLOCK, :] - shifted)
    grow = jnp.exp(lc)

    def spread(cols, a):
        left = lax.broadcasted_iota(jnp.int32, (cols.shape[0], 2 * hd), 1) < hd
        return jnp.where(left, cols[:, a : a + 1], cols[:, a + 1 : a + 2])

    def arrived(i, ref, waits, own_copy):
        for w in waits:
            w.wait_recv()
        own_copy.wait()

        @pl.when(ctx < nctx - 1)
        def _():
            halo(i, ref).start()

        @pl.when(ctx > 0)
        def _():
            halo(i, ref).wait_recv()

    for g in range(groups):
        for a in range(0, per, 2):
            ex[g, :, a * hd : (a + 2) * hd] = spread(grow, g * per + a)

    arrived(0, praw, [p_copy(k, to(k), source(k)) for k in range(1, n)], own[0])
    conv_rows(praw, pc, w_pairs, me * pw, pw, store_plain)
    bts = []
    for g in range(groups):
        bt = pc[:, 2 * g * st : (2 * g + 1) * st].astype(F32).T.astype(BF)
        bts.append(bt)
        raw_scores = jnp.dot(
            pc[:, (2 * g + 1) * st : (2 * g + 2) * st], bt, preferred_element_type=F32)
        scores[g] = jnp.where(lower, raw_scores, 0.0)

    def prepare(g):
        arrived(1 + g, xraw.at[g],
                [x_copy(g, k, to(k), source(k)) for k in range(1, n)], own[1 + g])
        conv_rows(xraw.at[g], xc.at[g], w_inner, me * width + g * gw, gw, store_plain)
        for p in range(pieces):
            parts = []
            for a in range(p * WIDE // hd, (p + 1) * WIDE // hd, 2):
                x = xc[g, :, a * hd : (a + 2) * hd].astype(F32)
                parts.append((x * spread(tail, g * per + a)).astype(BF))
            weighted = jnp.concatenate(parts, axis=1)
            local[g, p] = jnp.dot(bts[g], weighted, preferred_element_type=F32)

            @pl.when(ctx == 0)
            def _():
                cout[g, p] = local[g, p].astype(BF)
                if nctx > 1:
                    chain(g, p).start()

    half = BLOCK // 2

    def intra(g, a):
        x = xc[g, :, a * hd : (a + 2) * hd]
        top, low = [], []
        for b in (a, a + 1):
            h = g * per + b
            col = lc[:, h : h + 1]
            row = shifted_t[h : h + 1, :]
            w0 = scores[g, :half, :half] * jnp.exp(jnp.minimum(col[:half] - row[:, :half], 30.0))
            top.append(jnp.dot(w0.astype(BF), x[:half], preferred_element_type=F32))
            w1 = scores[g, half:, :] * jnp.exp(jnp.minimum(col[half:] - row, 30.0))
            low.append(jnp.dot(w1.astype(BF), x, preferred_element_type=F32))
        left = lax.broadcasted_iota(jnp.int32, (half, 2 * hd), 1) < hd
        gain = spread(skip_gain[...], g * per + a)
        xf = x.astype(F32) * gain
        mixed[g, :half, a * hd : (a + 2) * hd] = jnp.where(left, top[0], top[1]) + xf[:half]
        mixed[g, half:, a * hd : (a + 2) * hd] = jnp.where(left, low[0], low[1]) + xf[half:]

    def serve(g, p):
        cols = slice(p * WIDE, (p + 1) * WIDE)

        @pl.when(ctx > 0)
        def _():
            chain(g, p).wait_recv()
            held = cin[g, p]

            @pl.when(ctx < nctx - 1)
            def _():
                decay = ex[g, BLOCK - 1 : BLOCK, cols]
                cout[g, p] = (decay * held.astype(F32) + local[g, p]).astype(BF)
                chain(g, p).start()

            cmat = pc[:, (2 * g + 1) * st : (2 * g + 2) * st]
            carried = jnp.dot(cmat, held, preferred_element_type=F32)
            mixed[g, :, cols] = mixed[g, :, cols] + carried * ex[g, :, cols]

    def work(g):
        for p in range(pieces):
            for a in range(p * WIDE // hd, (p + 1) * WIDE // hd, 2):
                intra(g, a)
            serve(g, p)

    own_out = []

    def finish(g):
        for k in list(range(1, n)) + [0]:
            who = to(k)
            rs = pl.ds(pl.multiple_of(who * rows, rows), rows)
            ssq = jnp.zeros((rows, 1), F32)
            for p in range(pieces):
                cols = slice(p * WIDE, (p + 1) * WIDE)
                z = gate[rs, g * gw + p * WIDE : g * gw + (p + 1) * WIDE].astype(F32)
                gated = mixed[g, rs, cols] * silu(z)
                mixed[g, rs, cols] = gated
                ssq = ssq + jnp.sum(gated * gated, axis=1, keepdims=True)
            inv = lax.rsqrt(ssq / gw + 1e-05)
            for p in range(pieces):
                cols = slice(p * WIDE, (p + 1) * WIDE)
                gain = norm_gain[:, g * gw + p * WIDE : g * gw + (p + 1) * WIDE]
                outbuf[g, rs, cols] = (mixed[g, rs, cols] * inv * gain).astype(BF)
            if k:
                o_copy(g, k, who, me).start()
            else:
                c = pltpu.make_async_copy(
                    outbuf.at[g, rs, :],
                    out.at[:, pl.ds(pl.multiple_of(me * width + g * gw, 128), gw)], olsem.at[g])
                c.start()
                own_out.append(c)

    gate_copy.wait()
    prepare(0)
    work(0)
    for g in range(1, groups):
        prepare(g)
        finish(g - 1)
        work(g)
    finish(groups - 1)

    for k in range(1, n):
        p_copy(k, to(k), me).wait_send()
        for g in range(groups):
            x_copy(g, k, to(k), me).wait_send()
            o_copy(g, k, to(k), me).wait_send()
            o_copy(g, k, to(k), source(k)).wait_recv()
    for c in own_out:
        c.wait()

    @pl.when(ctx < nctx - 1)
    def _():
        halo(0, praw).wait_send()
        for g in range(groups):
            halo(1 + g, xraw.at[g]).wait_send()
            for p in range(pieces):
                chain(g, p).wait_send()


def on_device(
    inner_raw, pairs_raw, gate_raw, step_raw, step_bias, rate_log,
    skip_gain, conv_inner, conv_pairs, norm_gain,
):
    n = lax.axis_size("head")
    nctx = lax.axis_size("context")
    rows, full = inner_raw.shape
    width = gate_raw.shape[1]
    heads = step_raw.shape[1]
    groups = pairs_raw.shape[1] // n
    st = pairs_raw.shape[3]
    pw = groups * 2 * st
    gw = width // groups
    pieces = gw // WIDE
    pairs = pairs_raw.reshape(rows, -1)
    w_pairs = conv_pairs.reshape(conv_pairs.shape[0], -1)
    vm = pl.BlockSpec(memory_space=pltpu.VMEM)
    hbm = pl.BlockSpec(memory_space=pl.ANY)
    dma = pltpu.SemaphoreType.DMA
    return pl.pallas_call(
        functools.partial(kernel, n, nctx, groups, heads),
        out_shape=jax.ShapeDtypeStruct((rows, full), BF),
        in_specs=[hbm, hbm, hbm] + [vm] * 7,
        out_specs=hbm,
        scratch_shapes=[
            pltpu.VMEM((BLOCK, width), BF),
            pltpu.VMEM((groups, PAD + BLOCK, gw), BF),
            pltpu.VMEM((PAD + BLOCK, pw), BF),
            pltpu.VMEM((groups, BLOCK, gw), BF),
            pltpu.VMEM((BLOCK, pw), BF),
            pltpu.VMEM((groups, BLOCK, gw), F32),
            pltpu.VMEM((groups, BLOCK, gw), F32),
            pltpu.VMEM((groups, pieces, st, WIDE), F32),
            pltpu.VMEM((groups, BLOCK, BLOCK), F32),
            pltpu.VMEM((groups, pieces, st, WIDE), BF),
            pltpu.VMEM((groups, pieces, st, WIDE), BF),
            pltpu.VMEM((groups, BLOCK, gw), BF),
            dma((groups, n - 1)), dma((groups, n - 1)),
            dma((n - 1,)), dma((n - 1,)),
            dma((1 + groups,)),
            dma((1 + groups,)), dma((1 + groups,)),
            dma((groups, pieces)), dma((groups, pieces)),
            dma((groups, n - 1)), dma((groups, n - 1)),
            dma((groups,)),
            dma,
        ],
        compiler_params=pltpu.CompilerParams(
            collective_id=0, has_side_effects=True, vmem_limit_bytes=58 * 1024 * 1024),
        cost_estimate=pl.CostEstimate(
            flops=700_000_000, bytes_accessed=4_000_000, transcendentals=4_000_000),
        name="mixer",
    )(
        inner_raw, pairs, gate_raw, step_raw.T, step_bias[None, :], rate_log[None, :],
        skip_gain[None, :], conv_inner, w_pairs, norm_gain[None, :],
    )


def solution(mesh):
    placed = (
        P(("rollout", "context", "head"), None),
        P(("rollout", "context", "head"), None, None, None),
        P(("rollout", "context"), "head"),
        P(("rollout", "context"), "head"),
        P("head"),
        P("head"),
        P("head"),
        P(),
        P(),
        P("head"),
    )
    return jax.shard_map(
        on_device,
        mesh=mesh,
        in_specs=placed,
        out_specs=P(("rollout", "context", "head"), None),
        check_vma=False,
    )
```
